32 devices in a mesh: dp: 4 (over y, x), chan: 8 (over z, core).
Axes of the slice: x: 2, y: 2, z: 4, core: 2. Of those that a mesh axis runs over, the one named last changes fastest.
Arguments:
- block_input: float32 [320, 64, 768], P('chan', 'dp'), may hold values from -48 to 48
- cotangent: float32 [320, 64, 768], P('chan', 'dp'), may hold values from -12 to 12
- canvas_rows: int32 [4], replicated, may hold values from 1 to 50, 64 in all
- square_weights: float32 [3, 320, 320], P(None, 'chan'), may hold values from -0.3125 to 0.3125
- square_momenta: float32 [3, 320, 320], P(None, 'chan'), may hold values from -3591.5806 to 3591.5806
- up_weight: float32 [1280, 320], P('chan'), may hold values from -0.3125 to 0.3125
- up_momentum: float32 [1280, 320], P('chan'), may hold values from -3591.5806 to 3591.5806
- down_weight: float32 [320, 1280], P(None, 'chan'), may hold values from -0.15625 to 0.15625
- down_momentum: float32 [320, 1280], P(None, 'chan'), may hold values from -3591.5806 to 3591.5806
- narrow_vectors: float32 [12, 320], P(None, 'chan'), may hold values from -2.4 to 2.4, as said below
- narrow_momenta: float32 [12, 320], P(None, 'chan'), may hold values from -384 to 384
- wide_vectors: float32 [2, 1280], P(None, 'chan'), may hold values from -6 to 6
- wide_momenta: float32 [2, 1280], P(None, 'chan'), may hold values from -384 to 384
- lka_kernels: float32 [320, 74], P('chan'), may hold values from -1 to 1
- lka_momenta: float32 [320, 74], P('chan'), may hold values from -384 to 384
- mlp_kernel: float32 [1280, 9], P('chan'), may hold values from -2 to 2
- mlp_momentum: float32 [1280, 9], P('chan'), may hold values from -384 to 384
Outputs:
- block_output: float32 [320, 64, 768], P('chan', 'dp')
- input_grad: float32 [320, 64, 768], P('chan', 'dp')
- new_square_weights: float32 [3, 320, 320], P(None, 'chan')
- new_square_momenta: float32 [3, 320, 320], P(None, 'chan')
- new_up_weight: float32 [1280, 320], P('chan')
- new_up_momentum: float32 [1280, 320], P('chan')
- new_down_weight: float32 [320, 1280], P(None, 'chan')
- new_down_momentum: float32 [320, 1280], P(None, 'chan')
- new_narrow_vectors: float32 [12, 320], P(None, 'chan')
- new_narrow_momenta: float32 [12, 320], P(None, 'chan')
- new_wide_vectors: float32 [2, 1280], P(None, 'chan')
- new_wide_momenta: float32 [2, 1280], P(None, 'chan')
- new_lka_kernels: float32 [320, 74], P('chan')
- new_lka_momenta: float32 [320, 74], P('chan')
- new_mlp_kernel: float32 [1280, 9], P('chan')
- new_mlp_momentum: float32 [1280, 9], P('chan')
The draws below stay inside these ranges and needn't reach their ends.
Inputs may be any that keep to these rules, and one draw needn't show every extreme that they name: `canvas_rows`: the tallest canvas has exactly 50 rows; the heights sum to 64. `narrow_vectors`: rows 0 and 8 lie in 0.6 to 1.6, rows 7 and 11 in 0.4 to 1.2.
All inputs are finite; a program needn't handle non-finite values.
Results may differ from the reference program's by a relative error of at most 0.014.
Values may be sent and summed in bfloat16 or wider, within the bound.
No kernel may reach another device: no remote copies, remote signals or barrier semaphores. Data moves between devices by JAX's collectives and lax.ppermute only.
A program may use at most 256 MiB of HBM per device.

```python
import math
from functools import partial
import jax
import jax.numpy as jnp
import numpy as np
from jax import lax

C = 320
HID = 1280
ROWS = 16
WIDTH = 768
CANVASES = 4
SCHULZ_STEPS = 5
HEIGHT = 64
PIXELS = 49152


def row_factors(key, extent, low_end, high_end):
    return jnp.exp(jax.random.uniform(key, (extent,), jnp.float32, math.log(low_end), math.log(high_end)))


def trend_factors(key, array_shape, trend_dim):
    key_rows, key_cols = jax.random.split(key)
    extent = array_shape[trend_dim]
    rising = 0.5 + jnp.arange(extent, dtype=jnp.float32) / extent
    layout_shape = [1] * len(array_shape)
    layout_shape[trend_dim] = extent
    rowwise = row_factors(key_rows, array_shape[-2], 0.3, 3.0)
    colwise = row_factors(key_cols, array_shape[-1], 0.3, 3.0)
    return rising.reshape(layout_shape) * rowwise[:, None] * colwise[None, :]


def draw_block_input(key, part):
    key = jax.random.fold_in(key, 11)
    key_base, key_rows, key_cols = jax.random.split(key, 3)
    places = jnp.arange(HEIGHT, dtype=jnp.float32) / HEIGHT
    values = jnp.clip(jax.random.normal(key_base, (C, HEIGHT, WIDTH), jnp.float32), -5.0, 5.0)
    rising = 0.5 + places
    rowwise = rising * row_factors(key_rows, HEIGHT, 0.3, 3.0)
    colwise = row_factors(key_cols, WIDTH, 0.5, 2.0)
    return values * rowwise[None, :, None] * colwise[None, None, :]


def draw_cotangent(key, part):
    key = jax.random.fold_in(key, 12)
    key_base, key_rows = jax.random.split(key)
    places = jnp.arange(HEIGHT, dtype=jnp.float32) / HEIGHT
    values = jnp.clip(jax.random.normal(key_base, (C, HEIGHT, WIDTH), jnp.float32), -4.0, 4.0)
    rising = 0.5 + places
    rowwise = rising * row_factors(key_rows, HEIGHT, 0.5, 2.0)
    return values * rowwise[None, :, None]


def draw_square_momenta(key, part):
    key = jax.random.fold_in(key, 13)
    key_base, key_scale = jax.random.split(key, 2)
    array_shape = (3, C, C)
    values = jnp.clip(jax.random.normal(key_base, array_shape, jnp.float32), -4.0, 4.0)
    return 0.3 * math.sqrt(PIXELS) * values * trend_factors(key_scale, array_shape, 1)


def draw_up_momentum(key, part):
    key = jax.random.fold_in(key, 14)
    key_base, key_scale = jax.random.split(key, 2)
    array_shape = (HID, C)
    values = jnp.clip(jax.random.normal(key_base, array_shape, jnp.float32), -4.0, 4.0)
    return 0.3 * math.sqrt(PIXELS) * values * trend_factors(key_scale, array_shape, 0)


def draw_down_momentum(key, part):
    key = jax.random.fold_in(key, 15)
    key_base, key_scale = jax.random.split(key, 2)
    array_shape = (C, HID)
    values = jnp.clip(jax.random.normal(key_base, array_shape, jnp.float32), -4.0, 4.0)
    return 0.3 * math.sqrt(PIXELS) * values * trend_factors(key_scale, array_shape, 1)


def draw_narrow_vectors(key, part):
    key = jax.random.fold_in(key, 16)
    key_base, key_gain, key_scale = jax.random.split(key, 3)
    biases = 0.4 * jnp.clip(jax.random.normal(key_base, (12, C), jnp.float32), -6.0, 6.0)
    gains = jnp.exp(jax.random.uniform(key_gain, (12, C), jnp.float32, math.log(0.6), math.log(1.6)))
    scales = jnp.exp(jax.random.uniform(key_scale, (12, C), jnp.float32, math.log(0.4), math.log(1.2)))
    row_kinds = jnp.arange(12, dtype=jnp.int32)
    is_gain = ((row_kinds == 0) | (row_kinds == 8))[:, None]
    is_scale = ((row_kinds == 7) | (row_kinds == 11))[:, None]
    return jnp.where(is_gain, gains, jnp.where(is_scale, scales, biases))


def shard_levels(key, shape, shards, smallest, largest):
    level, own = 1.0, jax.random.fold_in(key, 6)
    for position, blocks in shards:
        heights = jnp.exp(jax.random.uniform(jax.random.fold_in(own, position), (blocks,), jnp.float32, smallest / len(shards), largest / len(shards)))
        level = level * jnp.repeat(heights, shape[position] // blocks).reshape([-1 if axis == position else 1 for axis in range(len(shape))])
    return level


def split_up(count, total, limit, lean):
    loads = [(1 << 20) // math.isqrt(rank ** lean) + 1 for rank in range(2, count + 1)]
    rest, given = total - limit - (count - 1), [1] * (count - 1)
    while rest > 0:
        movable = [i for i in range(count - 1) if given[i] < limit]
        pool, left = sum([loads[i] for i in movable]), rest
        for i in movable:
            more = min(limit - given[i], max(1, left * loads[i] // pool), rest)
            given[i] = given[i] + more
            rest = rest - more
    return np.array([limit] + given)


def ragged_sizes(own_key, number_of, total, most, lean):
    if number_of == 2:
        one = jax.random.randint(own_key, (), max(1, total - most), min(most, total - 1) + 1)
        return jnp.stack([one, total - one])
    sizes = jnp.asarray(split_up(number_of, total, most, lean), jnp.int32)
    twos = (number_of - 1) // 2
    source_of, receiver = sizes[1:1 + 2 * twos:2], sizes[2:2 + 2 * twos:2]
    margin = jnp.minimum(source_of - 1, most - receiver)
    shifted = jax.random.randint(jax.random.fold_in(own_key, 1), (twos,), 0, 1 << 20) % (margin + 1)
    sizes = sizes.at[1:1 + 2 * twos:2].set(source_of - shifted).at[2:2 + 2 * twos:2].set(receiver + shifted)
    return sizes[jax.random.permutation(jax.random.fold_in(own_key, 2), number_of)]


def scatter_about(own_key, shape, width, reach, cuts=(), kind=jnp.bfloat16):
    level = shard_levels(own_key, shape, cuts, -0.22, 0.18) if cuts else 1.0
    array = jax.random.normal(own_key, shape, jnp.float32) * width * level
    return jnp.minimum(jnp.maximum(array, -reach), reach).astype(kind)


def setup_inputs(seed: int = 0) -> dict:
    streams_of = jax.random.split(jax.random.key(seed), 18)
    block_input = draw_block_input(jax.random.fold_in(streams_of[17], 71), 0)
    cotangent = draw_cotangent(jax.random.fold_in(streams_of[17], 71), 0)
    canvas_rows = ragged_sizes(streams_of[2], CANVASES, 4 * ROWS, 3 * ROWS + 2, 1).astype(jnp.int32)
    square_weights = scatter_about(streams_of[3], (3, C, C), C ** -0.5, 0.3125, ((1, 8),), jnp.float32)
    square_momenta = draw_square_momenta(jax.random.fold_in(streams_of[17], 71), 0)
    up_weight = scatter_about(streams_of[5], (HID, C), C ** -0.5, 0.3125, ((0, 8),), jnp.float32)
    up_momentum = draw_up_momentum(jax.random.fold_in(streams_of[17], 71), 0)
    down_weight = scatter_about(streams_of[7], (C, HID), HID ** -0.5, 0.15625, ((1, 8),), jnp.float32)
    down_momentum = draw_down_momentum(jax.random.fold_in(streams_of[17], 71), 0)
    narrow_vectors = draw_narrow_vectors(jax.random.fold_in(streams_of[17], 71), 0)
    narrow_momenta = scatter_about(streams_of[10], (12, C), (0.3 * PIXELS ** 0.5), 384.0, ((1, 8),), jnp.float32)
    wide_vectors = scatter_about(streams_of[11], (2, HID), 0.4, 6.0, ((1, 8),), jnp.float32)
    wide_momenta = scatter_about(streams_of[12], (2, HID), (0.3 * PIXELS ** 0.5), 384.0, ((1, 8),), jnp.float32)
    lka_kernels = scatter_about(streams_of[13], (C, 74), 36 ** -0.5, 1.0, ((0, 8),), jnp.float32)
    lka_momenta = scatter_about(streams_of[14], (C, 74), (0.3 * PIXELS ** 0.5), 384.0, ((0, 8),), jnp.float32)
    mlp_kernel = scatter_about(streams_of[15], (HID, 9), 9 ** -0.5, 2.0, ((0, 8),), jnp.float32)
    mlp_momentum = scatter_about(streams_of[16], (HID, 9), (0.3 * PIXELS ** 0.5), 384.0, ((0, 8),), jnp.float32)
    return dict(block_input=block_input, cotangent=cotangent, canvas_rows=canvas_rows, square_weights=square_weights, square_momenta=square_momenta, up_weight=up_weight, up_momentum=up_momentum, down_weight=down_weight, down_momentum=down_momentum, narrow_vectors=narrow_vectors, narrow_momenta=narrow_momenta, wide_vectors=wide_vectors, wide_momenta=wide_momenta, lka_kernels=lka_kernels, lka_momenta=lka_momenta, mlp_kernel=mlp_kernel, mlp_momentum=mlp_momentum)


EPSILON = 1e-05
ORDER_ONE = 3.4445
ORDER_THREE = -4.775
ORDER_FIVE = 2.0315
MATRIX_MOMENTUM = 0.95
VECTOR_MOMENTUM = 0.9
MATRIX_RATE = 0.3
VECTOR_RATE = 0.2
WEIGHT_DECAY = 0.01
HIGHEST = lax.Precision.HIGHEST

@jax.custom_vjp
def low(v):
    return lax.optimization_barrier(v.astype(jnp.bfloat16)).astype(jnp.float32)

@jax.custom_vjp
def low_back(v):
    return v

def low_keep(v):
    return (low(v), None)

def low_pass(kept, grad):
    return (grad,)

def back_keep(v):
    return (v, None)

def back_low(kept, grad):
    return (low(grad),)
low.defvjp(low_keep, low_pass)
low_back.defvjp(back_keep, back_low)

def canvas_of(canvas_rows, positions):
    canvas_ends = jnp.cumsum(canvas_rows)
    return lax.optimization_barrier(jnp.sum((positions[:, None] >= canvas_ends[None, :]).astype(jnp.int32), axis=1))

def tap_masks(canvas_rows, first_row, row_count, height, taps_side, dilation):
    row_index = first_row + jnp.arange(row_count, dtype=jnp.int32)
    own_canvas = canvas_of(canvas_rows, row_index)
    row_masks = []
    for tap_row in range(taps_side):
        neighbour = row_index + (tap_row - taps_side // 2) * dilation
        inside = (neighbour >= 0) & (neighbour < height)
        same_canvas = canvas_of(canvas_rows, neighbour) == own_canvas
        row_masks.append((inside & same_canvas).astype(jnp.float32))
    return row_masks

def conv_taps(feature, kernel, row_masks, taps_side, dilation):
    halo_width = taps_side // 2 * dilation
    height_here = feature.shape[1]
    width_here = feature.shape[2]
    padded = jnp.pad(feature, ((0, 0), (halo_width, halo_width), (halo_width, halo_width)))
    summed = jnp.zeros_like(feature)
    for tap_row in range(taps_side):
        band_rows = padded[:, tap_row * dilation:tap_row * dilation + height_here, :] * row_masks[tap_row][None, :, None]
        for tap_col in range(taps_side):
            window = band_rows[:, :, tap_col * dilation:tap_col * dilation + width_here]
            summed = summed + kernel[:, tap_row * taps_side + tap_col][:, None, None] * window
    return summed

def batch_norm(feature, gain, shift):
    mean_value = lax.optimization_barrier(jnp.mean(feature, axis=(1, 2), keepdims=True))
    variance = lax.optimization_barrier(jnp.mean(feature * feature, axis=(1, 2), keepdims=True)) - mean_value * mean_value
    return (feature - mean_value) * lax.rsqrt(variance + EPSILON) * gain[:, None, None] + shift[:, None, None]

def pointwise(weight, feature, bias):
    channels = feature.shape[0]
    flat_in = low(feature).reshape(channels, feature.shape[1] * feature.shape[2])
    product = jnp.dot(low(weight), flat_in, precision=HIGHEST)
    shaped = product.reshape((weight.shape[0], feature.shape[1], feature.shape[2]))
    return low_back(shaped + bias[:, None, None])

def block(block_input, square_weights, up_weight, down_weight, narrow_vectors, wide_vectors, lka_kernels, mlp_kernel, masks_five, masks_seven, masks_three):
    conv_five = jax.checkpoint(partial(conv_taps, taps_side=5, dilation=1))
    conv_seven = jax.checkpoint(partial(conv_taps, taps_side=7, dilation=3))
    conv_three = jax.checkpoint(partial(conv_taps, taps_side=3, dilation=1))

    def column(row_number):
        return narrow_vectors[row_number][:, None, None]
    normed_one = batch_norm(block_input, narrow_vectors[0], narrow_vectors[1])
    first = pointwise(square_weights[0], normed_one, narrow_vectors[2])
    gated_in = jax.nn.gelu(first, approximate=False)
    after_five = conv_five(gated_in, lka_kernels[:, 0:25], masks_five) + column(3)
    after_seven = conv_seven(after_five, lka_kernels[:, 25:74], masks_seven) + column(4)
    attention = pointwise(square_weights[1], after_seven, narrow_vectors[5])
    projected = pointwise(square_weights[2], gated_in * attention, narrow_vectors[6])
    middle = block_input + column(7) * (projected + normed_one)
    normed_two = batch_norm(middle, narrow_vectors[8], narrow_vectors[9])
    expanded = pointwise(up_weight, normed_two, wide_vectors[0])
    mixed = conv_three(expanded, mlp_kernel, masks_three) + wide_vectors[1][:, None, None]
    branch_two = pointwise(down_weight, jax.nn.gelu(mixed, approximate=False), narrow_vectors[10])
    return middle + column(11) * branch_two

def orthogonalize(momentum):
    norm_value = jnp.sqrt(lax.optimization_barrier(jnp.sum(momentum * momentum, axis=(1, 2), keepdims=True)))
    iterate = momentum / (norm_value + 1e-07)
    for iteration in range(SCHULZ_STEPS):
        gram_matrix = jnp.einsum('bij,bkj->bik', iterate, iterate, precision=HIGHEST)
        polynomial = ORDER_THREE * gram_matrix + ORDER_FIVE * jnp.einsum('bij,bjk->bik', gram_matrix, gram_matrix, precision=HIGHEST)
        iterate = ORDER_ONE * iterate + jnp.einsum('bij,bjk->bik', polynomial, iterate, precision=HIGHEST)
    return iterate

def reference(block_input, cotangent, canvas_rows, square_weights, square_momenta, up_weight, up_momentum, down_weight, down_momentum, narrow_vectors, narrow_momenta, wide_vectors, wide_momenta, lka_kernels, lka_momenta, mlp_kernel, mlp_momentum):
    masks_five = tap_masks(canvas_rows, 0, HEIGHT, HEIGHT, 5, 1)
    masks_seven = tap_masks(canvas_rows, 0, HEIGHT, HEIGHT, 7, 3)
    masks_three = tap_masks(canvas_rows, 0, HEIGHT, HEIGHT, 3, 1)

    def forward(*arguments):
        return block(*arguments, masks_five, masks_seven, masks_three)
    block_output, pullback = jax.vjp(forward, block_input, square_weights, up_weight, down_weight, narrow_vectors, wide_vectors, lka_kernels, mlp_kernel)
    input_grad, square_grad, up_grad, down_grad, narrow_grad, wide_grad, lka_grad, mlp_grad = pullback(cotangent)
    new_square_momenta = MATRIX_MOMENTUM * square_momenta + square_grad
    new_up_momentum = MATRIX_MOMENTUM * up_momentum + up_grad
    new_down_momentum = MATRIX_MOMENTUM * down_momentum + down_grad
    square_ortho = orthogonalize(new_square_momenta)
    up_ortho = orthogonalize(new_up_momentum.T[None])[0].T
    down_ortho = orthogonalize(new_down_momentum[None])[0]
    shrink = 1.0 - MATRIX_RATE * WEIGHT_DECAY
    new_square_weights = shrink * square_weights - MATRIX_RATE * square_ortho
    new_up_weight = shrink * up_weight - MATRIX_RATE * math.sqrt(max(1.0, HID / C)) * up_ortho
    new_down_weight = shrink * down_weight - MATRIX_RATE * math.sqrt(max(1.0, C / HID)) * down_ortho
    vector_step = VECTOR_RATE / math.sqrt(PIXELS)
    new_narrow_momenta = VECTOR_MOMENTUM * narrow_momenta + narrow_grad
    new_narrow_vectors = narrow_vectors - vector_step * new_narrow_momenta
    new_wide_momenta = VECTOR_MOMENTUM * wide_momenta + wide_grad
    new_wide_vectors = wide_vectors - vector_step * new_wide_momenta
    new_lka_momenta = VECTOR_MOMENTUM * lka_momenta + lka_grad
    new_lka_kernels = lka_kernels - vector_step * new_lka_momenta
    new_mlp_momentum = VECTOR_MOMENTUM * mlp_momentum + mlp_grad
    new_mlp_kernel = mlp_kernel - vector_step * new_mlp_momentum
    return (block_output, input_grad, new_square_weights, new_square_momenta, new_up_weight, new_up_momentum, new_down_weight, new_down_momentum, new_narrow_vectors, new_narrow_momenta, new_wide_vectors, new_wide_momenta, new_lka_kernels, new_lka_momenta, new_mlp_kernel, new_mlp_momentum)
```

```python
import functools
import math

import jax
import jax.numpy as jnp
import numpy as np
from jax import lax
from jax.experimental import pallas as pl
from jax.experimental.pallas import tpu as pltpu
from jax.sharding import PartitionSpec as P

C = 320
HID = 1280
SCHULZ_STEPS = 5
EPSILON = 1e-05
ORDER_ONE = 3.4445
ORDER_THREE = -4.775
ORDER_FIVE = 2.0315
MATRIX_MOMENTUM = 0.95
VECTOR_MOMENTUM = 0.9
MATRIX_RATE = 0.3
VECTOR_RATE = 0.2
WEIGHT_DECAY = 0.01
HIGHEST = lax.Precision.HIGHEST
BOTH = ("dp", "chan")
LANES = 128
SUB = 8
HIDDEN_TILE = 256
VMEM_LIMIT = 56 * 1024 * 1024
SIDE_WIDTH = 64
F32 = jnp.float32
BF16 = jnp.bfloat16


def lower(values):
    return values.astype(BF16)


def cost(microseconds):
    return pl.CostEstimate(
        flops=int(microseconds * 1e9), bytes_accessed=int(microseconds * 3e6), transcendentals=0
    )


def add_row(ref, row, values):
    ref[row : row + 1, :] = ref[row : row + 1, :] + jnp.sum(values, axis=0, keepdims=True)


def gelu_parts(values):
    cdf = 0.5 * (1.0 + lax.erf(values * 0.7071067811865476))
    slope = cdf + values * jnp.exp(-0.5 * values * values) * 0.3989422804014327
    return values * cdf, slope


def masks_kernel(columns, width, rows_ref, five_ref, seven_ref, three_ref, valid_ref):
    height = five_ref.shape[1]
    row = lax.broadcasted_iota(jnp.int32, (height, LANES), 0)

    def canvas(position):
        number = jnp.zeros((height, LANES), jnp.int32)
        end = 0
        for k in range(rows_ref.shape[0] - 1):
            end = end + rows_ref[k]
            number = number + jnp.where(position >= end, 1, 0)
        return number

    own = canvas(row)
    for ref, side, dilation in ((five_ref, 5, 1), (seven_ref, 7, 3), (three_ref, 3, 1)):
        for tap in range(side):
            other = row + (tap - side // 2) * dilation
            inside = (other >= 0) & (other < height) & (canvas(other) == own)
            ref[tap] = jnp.where(inside, 1.0, 0.0)
    count = valid_ref.shape[0]
    place = lax.broadcasted_iota(jnp.int32, (count, 1, LANES), 0) - (count - width) // 2
    place = place + rows_ref[rows_ref.shape[0] - 1] * width
    valid_ref[...] = jnp.where((place >= 0) & (place < columns), 1.0, 0.0)


def make_masks(canvas_rows, index, height, columns, width, ties):
    scalars = jnp.concatenate([canvas_rows, index[None].astype(jnp.int32)])
    kernel, tie_specs = tied(functools.partial(masks_kernel, columns, width), 1, ties)
    return pl.pallas_call(
        kernel,
        out_shape=[jax.ShapeDtypeStruct((k, height, LANES), F32) for k in (5, 7, 3)]
        + [jax.ShapeDtypeStruct((width + 18, 1, LANES), F32)],
        in_specs=[pl.BlockSpec(memory_space=pltpu.SMEM)] + tie_specs,
        out_specs=[pl.BlockSpec(memory_space=pltpu.VMEM)] * 4,
        cost_estimate=cost(1),
        name="masks",
    )(scalars, *ties)


def largest_divisor(number, most):
    for candidate in range(min(number, most), 0, -1):
        if number % candidate == 0:
            return candidate
    return 1


def roll_rows(values, shift):
    rows = values.shape[0]
    if shift % rows == 0:
        return values
    return pltpu.roll(values, shift % rows, 0)


def packed_rows(dtype):
    return SUB if dtype == F32 else 2 * SUB


def times_tap(tap, column):
    rows, lanes = column.shape
    each = packed_rows(column.dtype)
    return (tap[None] * column.reshape(rows // each, each, lanes)).reshape(rows, lanes)


def fold_rows(values):
    rows, lanes = values.shape
    each = packed_rows(values.dtype)
    values = values.reshape(rows // each, each, lanes)
    total = values[0]
    for k in range(1, rows // each):
        total = total + values[k]
    total = total.astype(F32)
    return total if each == SUB else total[:SUB] + total[SUB:]


def group_base(step, size, dilation):
    if dilation == 1:
        return step * size
    return (step // dilation) * (size * dilation) + step % dilation


UNROLL = 4


def run_groups(groups, step_body, carry):
    full = groups // UNROLL

    def chunk(index, carry):
        for u in range(UNROLL):
            carry = step_body(index * UNROLL + u, carry)
        return carry

    carry = lax.fori_loop(0, full, chunk, carry)
    for step in range(full * UNROLL, groups):
        carry = step_body(jnp.int32(step), carry)
    return carry


def conv_columns(load, tap, mask, side, dilation, columns, most, emit):
    size = largest_divisor(columns // dilation, most)

    def step_body(step, carry):
        base = group_base(step, size, dilation)
        totals = [None] * size
        for i in range(side):
            sums = [None] * size
            for c in range(size + side - 1):
                column = load(base + dilation * c)
                for j in range(side):
                    q = c - j
                    if 0 <= q < size:
                        term = times_tap(tap(i, j), column)
                        sums[q] = term if sums[q] is None else sums[q] + term
            offset = dilation * (i - side // 2)
            for q in range(size):
                term = sums[q].astype(F32)
                term = term if offset == 0 else mask(i) * roll_rows(term, -offset)
                totals[q] = term if totals[q] is None else totals[q] + term
        for q in range(size):
            emit(base + dilation * q, totals[q])
        return carry

    run_groups(columns // size, step_body, 0)


def tap_gradients(load_grad, load, mask, side, dilation, columns, most, store):
    size = largest_divisor(columns // dilation, most)
    lanes = LANES
    for i in range(side):
        offset = dilation * (i - side // 2)

        def step_body(step, sums, i=i, offset=offset):
            sums = list(sums)
            base = group_base(step, size, dilation)
            shifted = []
            for q in range(size):
                gradient = load_grad(base + dilation * q)
                if offset != 0:
                    moved = roll_rows(mask(i) * gradient.astype(F32), offset)
                    gradient = moved.astype(gradient.dtype)
                shifted.append(gradient)
            for c in range(size + side - 1):
                column = load(base + dilation * c)
                for j in range(side):
                    q = c - j
                    if 0 <= q < size:
                        sums[j] = sums[j] + fold_rows(shifted[q] * column)
            return tuple(sums)

        sums = run_groups(
            columns // size,
            step_body,
            tuple(jnp.zeros((SUB, lanes), F32) for _ in range(side)),
        )
        for j in range(side):
            store(i * side + j, jnp.sum(sums[j], axis=0, keepdims=True))


def spread_taps(kernel_ref, spread_ref, count):
    rows, lanes = spread_ref.shape[1:]
    for index in range(count):
        row = jnp.broadcast_to(kernel_ref[index : index + 1, :], (rows, lanes))
        spread_ref[index] = row.astype(spread_ref.dtype)


def join(target, pieces):
    place = 0
    for piece, first, count in pieces:
        target[place : place + count] = piece[first : first + count].astype(target.dtype)
        place += count


def attention_forward_kernel(
    width,
    left_ref,
    g_ref,
    right_ref,
    kernel_ref,
    bias_ref,
    five_ref,
    seven_ref,
    valid_ref,
    t5_ref,
    t7_ref,
    spread,
    gf,
):
    spread_taps(kernel_ref, spread, 74)
    join(gf, [(left_ref, 0, 11), (g_ref, 0, width), (right_ref, 0, 11)])
    bias_five = bias_ref[0:1, :]
    bias_seven = bias_ref[1:2, :]

    def emit_five(w, value):
        t5_ref[w] = lower((value + bias_five) * valid_ref[w])

    conv_columns(
        lambda w: gf[w],
        lambda i, j: spread[i * 5 + j],
        lambda i: five_ref[i],
        5,
        1,
        width + 18,
        3,
        emit_five,
    )

    def emit_seven(w, value):
        t7_ref[w] = lower(value + bias_seven)

    conv_columns(
        lambda w: t5_ref[w],
        lambda i, j: spread[25 + i * 7 + j],
        lambda i: seven_ref[i],
        7,
        3,
        width,
        2,
        emit_seven,
    )


def attention_backward_kernel(
    width,
    left_ref,
    d7_ref,
    right_ref,
    kernel_ref,
    five_ref,
    seven_ref,
    valid_ref,
    dg_ref,
    d5_ref,
    bias_ref,
    spread,
    d7,
    d5,
):
    spread_taps(kernel_ref, spread, 74)
    join(d7, [(left_ref, 0, 12), (d7_ref, 0, width), (right_ref, 0, 12)])

    def emit_five(w, value):
        d5[w] = lower(value * valid_ref[w + 6])

    conv_columns(
        lambda w: d7[w],
        lambda i, j: spread[25 + 48 - (i * 7 + j)],
        lambda i: seven_ref[i],
        7,
        3,
        width + 6,
        2,
        emit_five,
    )

    def emit_g(w, value):
        dg_ref[w] = value

    conv_columns(
        lambda w: d5[w + 1],
        lambda i, j: spread[24 - (i * 5 + j)],
        lambda i: five_ref[i],
        5,
        1,
        width,
        3,
        emit_g,
    )
    d5_ref[...] = d5[3 : 3 + width]
    sums = lax.fori_loop(
        0,
        width,
        lambda w, sums: sums + fold_rows(d5[w + 3].astype(F32)),
        jnp.zeros((SUB, LANES), F32),
    )
    bias_ref[0:1, :] = jnp.sum(sums, axis=0, keepdims=True)


def tap_seven_kernel(width, d7_ref, t5_ref, seven_ref, taps_ref):
    def store(index, value):
        taps_ref[index : index + 1, :] = value

    tap_gradients(
        lambda w: d7_ref[w], lambda w: t5_ref[w], lambda i: seven_ref[i], 7, 3, width, 2, store
    )


def tap_five_kernel(width, d5_ref, left_ref, g_ref, right_ref, five_ref, taps_ref, gf):
    join(gf, [(left_ref, 9, 2), (g_ref, 0, width), (right_ref, 0, 2)])

    def store(index, value):
        taps_ref[index : index + 1, :] = value

    tap_gradients(
        lambda w: d5_ref[w], lambda w: gf[w], lambda i: five_ref[i], 5, 1, width, 3, store
    )


def dot_nt(left, right):
    return lax.dot_general(left, right, (((1,), (1,)), ((), ())), preferred_element_type=F32)


def dot_nn(left, right):
    return lax.dot_general(left, right, (((1,), (0,)), ((), ())), preferred_element_type=F32)


def dot_tn(left, right):
    return lax.dot_general(left, right, (((0,), (0,)), ((), ())), preferred_element_type=F32)


def conv_three(load, tap, mask, size):
    totals = [None] * size
    for i in range(3):
        sums = [None] * size
        for c in range(size + 2):
            column = load(c)
            for j in range(3):
                q = c - j
                if 0 <= q < size:
                    term = times_tap(tap(i, j), column)
                    sums[q] = term if sums[q] is None else sums[q] + term
        for q in range(size):
            term = sums[q].astype(F32)
            term = term if i == 1 else mask(i) * roll_rows(term, 1 - i)
            totals[q] = term if totals[q] is None else totals[q] + term
    return totals


def mlp_kernel_body(
    width,
    height,
    mid_left,
    mid_ref,
    mid_right,
    cot_ref,
    totals_ref,
    vector_ref,
    pair_ref,
    bias_ref,
    kernel_ref,
    three_ref,
    valid_ref,
    ff_ref,
    dn2_ref,
    gup_ref,
    gdown_ref,
    sums_ref,
    spread,
    n2_ref,
    dff_ref,
    h,
    mixed,
    act,
    dh,
    ff,
    dn2,
    tap_acc,
    sum_acc,
    up_ref,
    downt_ref,
):
    tile, channels = up_ref.shape
    own = width * height
    step_id = pl.program_id(0)
    size = 2 if width % 2 == 0 else 1
    group = size * height
    parts = [slice(k * LANES, (k + 1) * LANES) for k in range(tile // LANES)]

    def rows_at(column, count=1):
        start = column * height
        if not isinstance(column, int):
            start = pl.multiple_of(start, height)
        return pl.ds(start, count * height)

    block = pair_ref.shape[1] // 2
    chunk = math.gcd(block, tile)
    for part in range(tile // chunk):
        row = step_id * tile + part * chunk
        place = lax.rem(row, block)
        here = slice(part * chunk, (part + 1) * chunk)
        for ref, start in ((up_ref, place), (downt_ref, place + block)):
            ref[here, :] = pair_ref[row // block, pl.ds(pl.multiple_of(start, chunk), chunk), :]
    spread_taps(kernel_ref, spread, 9)

    def second_statistics():
        totals = jnp.sum(totals_ref[...], axis=0) * (1.0 / (own * totals_ref.shape[0]))
        mean = totals[0:1, :]
        return mean, lax.rsqrt(totals[1:2, :] - mean * mean + EPSILON)

    @pl.when(step_id == 0)
    def _():
        mean, rstd = second_statistics()
        gain, shift, scale = vector_ref[8:9, :], vector_ref[9:10, :], vector_ref[11:12, :]

        def put_norm(column, values):
            unit = (values.astype(F32) - mean) * rstd
            n2_ref[rows_at(column), :] = lower(unit * gain + shift)

        def put_grad(column, values):
            dff_ref[rows_at(column), :] = lower(values.astype(F32) * scale)

        for w in range(2):
            put_norm(w, mid_left[w])
            put_norm(width + 2 + w, mid_right[w])
        put_grad(0, mid_left[2])
        put_grad(width + 1, mid_right[2])

        def own_column(w, carry):
            put_norm(w + 2, mid_ref[w])
            put_grad(w + 1, cot_ref[w])
            return carry

        lax.fori_loop(0, width, own_column, 0)
        n2_ref[rows_at(width + 4, size), :] = jnp.zeros((group, channels), BF16)
        act[0:group, :] = jnp.zeros((group, tile), BF16)
        dh[0:group, :] = jnp.zeros((group, tile), BF16)
        ff[...] = jnp.zeros_like(ff)
        dn2[...] = jnp.zeros_like(dn2)

    def expand(first, count):
        return dot_nt(n2_ref[rows_at(first, count), :], up_ref[...])

    def put_hidden(first, count, product):
        product = (product + bias_ref[0:1, :]).reshape(count, height, tile)
        for w in range(count):
            h[first + w] = lower(product[w] * valid_ref[first + w + 7, 0:1, 0:1])

    put_hidden(0, size + 2, expand(0, size + 2))

    def add_output(first):
        rows = rows_at(first, size)
        ff[rows, :] = ff[rows, :] + dot_nn(act[rows, :], downt_ref[...])

    def forward(step, carry):
        base = step * size
        ahead = expand(base + size + 2, size)
        back = dot_nt(dff_ref[rows_at(base, size), :], downt_ref[...])
        add_output(base)
        for lanes in parts:
            values = conv_three(
                lambda c: h[base + c, :, lanes],
                lambda i, j: spread[i * 3 + j, :, lanes],
                lambda i: three_ref[i],
                size,
            )
            for q in range(size):
                active, grade = gelu_parts(values[q] + bias_ref[1:2, lanes])
                act[rows_at(base + size + q), lanes] = lower(active)
                gradient = back[q * height : (q + 1) * height, lanes] * grade
                mixed[base + q, :, lanes] = lower(gradient * valid_ref[base + q + 8])
        put_hidden(base + size + 2, size, ahead)
        return carry

    groups = (width + 2) // size
    lax.fori_loop(0, groups, forward, 0)
    add_output(groups * size)
    tap_acc[...] = jnp.zeros_like(tap_acc)
    sum_acc[...] = jnp.zeros_like(sum_acc)

    def add_norm_grad(first):
        rows = rows_at(first, size)
        dn2[rows, :] = dn2[rows, :] + dot_nn(dh[rows, :], up_ref[...])

    def backward(step, carry):
        base = step * size
        add_norm_grad(base)
        for lanes in parts:
            values = conv_three(
                lambda c: mixed[base + c, :, lanes],
                lambda i, j: spread[8 - (i * 3 + j), :, lanes],
                lambda i: three_ref[i],
                size,
            )
            sums = [jnp.zeros((SUB, LANES), F32)] * 11
            shifted = []
            for q in range(size):
                low_value = lower(values[q])
                dh[rows_at(base + size + q), lanes] = low_value
                sums[9] = sums[9] + fold_rows(low_value.astype(F32))
                gradient = mixed[base + q + 1, :, lanes]
                wide_gradient = gradient.astype(F32)
                sums[10] = sums[10] + fold_rows(wide_gradient)
                moved = [lower(roll_rows(three_ref[i] * wide_gradient, i - 1)) for i in (0, 2)]
                shifted.append([moved[0], gradient, moved[1]])
            for c in range(size + 2):
                column = h[base + c + 1, :, lanes]
                for j in range(3):
                    q = c - j
                    if 0 <= q < size:
                        for i in range(3):
                            k = i * 3 + j
                            sums[k] = sums[k] + fold_rows(shifted[q][i] * column)
            for k in range(9):
                tap_acc[k, :, lanes] = tap_acc[k, :, lanes] + sums[k]
            for k in range(2):
                sum_acc[k, :, lanes] = sum_acc[k, :, lanes] + sums[9 + k]
        return carry

    lax.fori_loop(0, width // size, backward, 0)
    add_norm_grad(width)
    side = jnp.concatenate(
        [jnp.sum(sum_acc[...], axis=1), jnp.sum(tap_acc[...], axis=1), jnp.zeros((5, tile), F32)]
    )
    flip = (
        lax.broadcasted_iota(jnp.int32, (side.shape[0], SIDE_WIDTH), 0)
        == lax.broadcasted_iota(jnp.int32, (side.shape[0], SIDE_WIDTH), 1)
    ).astype(BF16)
    gup_ref[:, :channels] = lower(
        dot_tn(dh[group : group + own, :], n2_ref[2 * height : 2 * height + own, :])
    )
    gup_ref[:, channels:] = lower(dot_tn(lower(side), flip))
    first_own = group + height
    gdown_ref[:, :channels] = lower(
        dot_tn(act[first_own : first_own + own, :], dff_ref[height : height + own, :])
    )
    gdown_ref[:, channels:] = jnp.zeros((tile, SIDE_WIDTH), BF16)

    @pl.when(step_id == pl.num_programs(0) - 1)
    def _():
        mean, rstd = second_statistics()
        ff_ref[...] = ff[first_own : first_own + own, :]
        dn2_ref[...] = dn2[group : group + own, :]

        def column_sums(w, sums):
            rows = dn2[rows_at(w + size), :]
            unit = (mid_ref[w] - mean) * rstd
            shape = (height // SUB, SUB, channels)
            return (
                sums[0] + jnp.sum(rows.reshape(shape), axis=0),
                sums[1] + jnp.sum((rows * unit).reshape(shape), axis=0),
            )

        zero = jnp.zeros((SUB, channels), F32)
        sums = lax.fori_loop(0, width, column_sums, (zero, zero))
        sums = jnp.concatenate([jnp.sum(v, axis=0, keepdims=True) for v in sums])
        sums_ref[...] = jnp.broadcast_to(sums[None], sums_ref.shape)


def zero_first(*refs):
    @pl.when(pl.program_id(0) == 0)
    def _():
        for ref in refs:
            ref[...] = jnp.zeros_like(ref)


def flat(ref):
    return ref[...].reshape(ref.shape[0] * ref.shape[1], ref.shape[2])


def put_edges(values, shape, low_ref, high_ref):
    columns = lower(values).reshape(shape)
    reach = low_ref.shape[0]
    low_ref[...] = columns[:reach]
    high_ref[...] = columns[shape[0] - reach :]


def middle_kernel(
    unpack,
    t7_ref,
    g_ref,
    unit_ref,
    vector_ref,
    second_ref,
    third_ref,
    *rest,
):
    if unpack:
        got_ref, order_ref, q_ref, gq_ref, branch_ref, middle_ref, sums_ref, *rest = rest
        low_ref, high_ref, cot_ref = rest
        cot_ref[...] = lower(dot_nt(order_ref[...], got_ref[...])).reshape(cot_ref.shape)
    else:
        cot_ref, q_ref, gq_ref, branch_ref, middle_ref, sums_ref, low_ref, high_ref = rest
    zero_first(sums_ref)
    shape = unit_ref.shape
    row = lambda k: vector_ref[k : k + 1, :]
    attention = dot_nt(flat(t7_ref), second_ref[...]) + row(3)
    gated = lower(flat(g_ref) * attention)
    projected = dot_nt(gated, third_ref[...]) + row(4)
    unit = flat(unit_ref)
    branch = projected + (unit * row(1) + row(2))
    middle = unit * row(0) + row(5) * branch
    q_ref[...] = attention.reshape(shape)
    gq_ref[...] = gated.reshape(shape)
    branch_ref[...] = branch.reshape(shape)
    middle_ref[...] = middle.reshape(shape)
    columns = lower(middle).reshape(shape)
    low_ref[:2] = columns[:2]
    low_ref[2] = cot_ref[0]
    high_ref[:2] = columns[shape[0] - 2 :]
    high_ref[2] = cot_ref[shape[0] - 1]
    sums = [jnp.sum(v, axis=0, keepdims=True) for v in (middle, middle * middle)]
    sums_ref[...] = sums_ref[...] + jnp.concatenate(sums)[None]


def put_blocks(out_ref, values, shape, order_ref):
    if order_ref is None:
        out_ref[...] = lower(values).reshape(shape)
    else:
        out_ref[...] = lower(dot_tn(lower(values), order_ref[...]))


def output_kernel(ff_ref, branch_ref, cot_ref, vector_ref, *rest):
    order_ref, out_ref, sums_ref = rest if len(rest) == 3 else (None,) + rest
    zero_first(sums_ref)
    row = lambda k: vector_ref[k : k + 1, :]
    ff = flat(ff_ref) + row(1)
    cot = flat(cot_ref).astype(F32)
    put_blocks(out_ref, row(0) * flat(branch_ref) + row(2) * ff, ff_ref.shape, order_ref)
    add_row(sums_ref, 0, cot * ff)
    add_row(sums_ref, 1, lower(cot * row(2)).astype(F32))


def branch_kernel(
    edges,
    dn2_ref,
    middle_ref,
    cot_ref,
    branch_ref,
    gq_ref,
    g_ref,
    t7_ref,
    totals_ref,
    norm_sums_ref,
    vector_ref,
    second_ref,
    third_ref,
    grad_ref,
    gated_ref,
    d7_ref,
    w2_ref,
    w3_ref,
    sums_ref,
    *rest,
):
    edge_refs, (acc2, acc3) = rest[:-2], rest[-2:]
    zero_first(sums_ref, acc2, acc3)
    shape = dn2_ref.shape
    channels = shape[2]
    row = lambda k: vector_ref[k : k + 1, :]
    part = 1.0 / (shape[0] * ROWS * pl.num_programs(0) * totals_ref.shape[0])
    totals = jnp.sum(totals_ref[...], axis=0) * part
    mean = totals[0:1, :]
    rstd = lax.rsqrt(totals[1:2, :] - mean * mean + EPSILON)
    norm_sums = jnp.sum(norm_sums_ref[...], axis=0)
    gain = row(8)
    unit = (flat(middle_ref) - mean) * rstd
    means = norm_sums * part
    norm_grad = (rstd * gain) * (flat(dn2_ref) - means[0:1, :] - unit * means[1:2, :])
    grad_middle = flat(cot_ref).astype(F32) + norm_grad
    grad_ref[...] = norm_grad.reshape(shape)
    add_row(sums_ref, 0, grad_middle * flat(branch_ref))
    low_three = lower(grad_middle * row(7))
    add_row(sums_ref, 1, low_three.astype(F32))
    back_gated = dot_nn(low_three, third_ref[...])
    gated_ref[...] = back_gated.reshape(shape)
    acc3[...] = acc3[...] + dot_tn(low_three, flat(gq_ref))
    low_two = lower(back_gated * flat(g_ref))
    add_row(sums_ref, 2, low_two.astype(F32))
    back_seven = dot_nn(low_two, second_ref[...])
    acc2[...] = acc2[...] + dot_tn(low_two, flat(t7_ref))
    add_row(sums_ref, 3, back_seven)
    d7_ref[...] = lower(back_seven).reshape(shape)
    if edges:
        put_edges(back_seven, shape, *edge_refs)
    sums_ref[4:6, :] = norm_sums

    @pl.when(pl.program_id(0) == pl.num_programs(0) - 1)
    def _():
        blank = jnp.zeros((channels, SIDE_WIDTH), BF16)
        for ref, acc in ((w2_ref, acc2), (w3_ref, acc3)):
            ref[:, :channels] = lower(acc[...])
            ref[:, channels:] = blank


def last_kernel(
    grid_shape,
    back_ref,
    gated_ref,
    q_ref,
    slope_ref,
    unit_ref,
    grad_ref,
    cot_ref,
    vector_ref,
    rstd_ref,
    first_ref,
    out_sums,
    branch_sums,
    bias_three,
    five_part,
    seven_part,
    *rest,
):
    order_ref, out_ref, rows_ref, w1, sums, vectors, rows = (
        rest if len(rest) == 7 else (None,) + rest
    )
    zero_first(w1, sums)
    row = lambda k: vector_ref[k : k + 1, :]
    unit = flat(unit_ref)
    norm_grad = flat(grad_ref)
    low_one = lower((flat(gated_ref) * flat(q_ref) + flat(back_ref)) * flat(slope_ref))
    add_row(sums, 2, low_one.astype(F32))
    grad_branch = (flat(cot_ref).astype(F32) + norm_grad) * row(7)
    grad_normed = grad_branch + dot_nn(low_one, first_ref[...])
    w1[...] = w1[...] + dot_tn(low_one, lower(unit * row(0) + row(1)))
    add_row(sums, 1, grad_normed)
    add_row(sums, 0, grad_normed * unit)
    scale = rstd_ref[...] * row(0)
    put_blocks(out_ref, norm_grad + scale * grad_normed, unit_ref.shape, order_ref)

    @pl.when(pl.program_id(0) == pl.num_programs(0) - 1)
    def _():
        dp, chan, local_chans, each, few = grid_shape
        vectors[...] = jnp.zeros_like(vectors)
        vectors[0:3, :] = sums[0:3, :]
        vectors[3:4, :] = bias_three[...]
        for k in range(4):
            vectors[4 + k : 5 + k, :] = branch_sums[3 - k : 4 - k, :]
        vectors[10:11, :] = out_sums[1:2, :]
        vectors[11:12, :] = out_sums[0:1, :]
        vectors[12:37, :] = five_part[...]
        vectors[37:86, :] = seven_part[...]
        rows[...] = jnp.zeros_like(rows)
        for d in range(dp):
            count = max(0, min(each, local_chans - d * each))
            for k in range(chan):
                i = d * chan + k
                if count:
                    first = k * local_chans + d * each
                    rows[i, 0:count, :] = w1[first : first + count, :]
                rows[i, each : each + few, :] = vectors[i * few : (i + 1) * few, :]
        rows_ref[...] = lower(rows[...])


def lane_spec(shape):
    if len(shape) == 2:
        return pl.BlockSpec((shape[0], LANES), lambda l: (0, l))
    return pl.BlockSpec((shape[0], shape[1], LANES), lambda l: (0, 0, l))


def whole_spec(shape):
    zeros = (0,) * len(shape)
    return pl.BlockSpec(shape, lambda l: zeros)


def tied(kernel, count, ties):
    specs = [pl.BlockSpec(memory_space=pl.ANY)] * len(ties)
    if not ties:
        return kernel, specs
    return lambda *refs: kernel(*refs[:count], *refs[count + len(ties) :]), specs


def lane_call(kernel, inputs, outputs, scratch, microseconds, name, ties=()):
    channels = outputs[0].shape[-1]
    kernel, tie_specs = tied(kernel, len(inputs), ties)
    return pl.pallas_call(
        kernel,
        grid=(pl.cdiv(channels, LANES),),
        in_specs=[lane_spec(v.shape) if lanes else whole_spec(v.shape) for v, lanes in inputs]
        + tie_specs,
        out_specs=[lane_spec(v.shape) for v in outputs],
        out_shape=outputs,
        scratch_shapes=scratch,
        compiler_params=pltpu.CompilerParams(vmem_limit_bytes=VMEM_LIMIT),
        cost_estimate=cost(microseconds),
        name=name,
    )(*[v for v, _ in inputs], *ties)


def attention_forward(g_parts, taps, biases, five, seven, valid):
    width, height, channels = g_parts[1].shape
    return lane_call(
        functools.partial(attention_forward_kernel, width),
        [(v, True) for v in (*g_parts, taps, biases)] + [(v, False) for v in (five, seven, valid)],
        [
            jax.ShapeDtypeStruct((width + 18, height, channels), BF16),
            jax.ShapeDtypeStruct((width, height, channels), BF16),
        ],
        [
            pltpu.VMEM((74, 2 * SUB, LANES), BF16),
            pltpu.VMEM((width + 22, height, LANES), BF16),
        ],
        23,
        "attention_forward",
    )


def attention_backward(d7_parts, taps, five, seven, valid, ties):
    width, height, channels = d7_parts[1].shape
    return lane_call(
        functools.partial(attention_backward_kernel, width),
        [(v, True) for v in (*d7_parts, taps)] + [(v, False) for v in (five, seven, valid)],
        [
            jax.ShapeDtypeStruct((width, height, channels), F32),
            jax.ShapeDtypeStruct((width, height, channels), BF16),
            jax.ShapeDtypeStruct((1, channels), F32),
        ],
        [
            pltpu.VMEM((74, 2 * SUB, LANES), BF16),
            pltpu.VMEM((width + 24, height, LANES), BF16),
            pltpu.VMEM((width + 6, height, LANES), BF16),
        ],
        21,
        "attention_backward",
        ties,
    )


def tap_sums_seven(d7, t5_ext, seven, ties):
    width, height, channels = d7.shape
    return lane_call(
        functools.partial(tap_seven_kernel, width),
        [(d7, True), (t5_ext, True), (seven, False)],
        [jax.ShapeDtypeStruct((49, channels), F32)],
        [],
        16,
        "tap_sums_seven",
        ties,
    )[0]


def tap_sums_five(d5, g_parts, five, ties):
    width, height, channels = d5.shape
    return lane_call(
        functools.partial(tap_five_kernel, width),
        [(v, True) for v in (d5, *g_parts)] + [(five, False)],
        [jax.ShapeDtypeStruct((25, channels), F32)],
        [pltpu.VMEM((width + 4, height, LANES), BF16)],
        7,
        "tap_sums_five",
        ties,
    )[0]


def mlp_both(mid_parts, cot, totals, vectors, pair, biases, taps, three, valid):
    width, height, channels = mid_parts[1].shape
    hidden = pair.shape[0] * pair.shape[1] // 2
    tile = HIDDEN_TILE
    own = width * height
    size = 2 if width % 2 == 0 else 1

    def rows_spec(columns):
        return pl.BlockSpec((tile, columns), lambda t: (t, 0))

    def lanes_spec(rows):
        return pl.BlockSpec((rows, tile), lambda t: (0, t))

    whole = [*mid_parts, cot, totals, vectors, pair]
    wide = channels + SIDE_WIDTH
    return pl.pallas_call(
        functools.partial(mlp_kernel_body, width, height),
        grid=(hidden // tile,),
        in_specs=[whole_spec(v.shape) for v in whole]
        + [
            lanes_spec(2),
            lanes_spec(9),
            whole_spec(three.shape),
            whole_spec(valid.shape),
        ],
        out_specs=[
            whole_spec((own, channels)),
            whole_spec((own, channels)),
            rows_spec(wide),
            rows_spec(wide),
            whole_spec(totals.shape),
        ],
        out_shape=[
            jax.ShapeDtypeStruct((own, channels), F32),
            jax.ShapeDtypeStruct((own, channels), F32),
            jax.ShapeDtypeStruct((hidden, wide), BF16),
            jax.ShapeDtypeStruct((hidden, wide), BF16),
            jax.ShapeDtypeStruct(totals.shape, F32),
        ],
        scratch_shapes=[
            pltpu.VMEM((9, 2 * SUB, tile), BF16),
            pltpu.VMEM(((width + 4 + size) * height, channels), BF16),
            pltpu.VMEM(((width + 2) * height, channels), BF16),
            pltpu.VMEM((width + 4 + size, height, tile), BF16),
            pltpu.VMEM((width + 2, height, tile), BF16),
            pltpu.VMEM(((width + 2 + size) * height, tile), BF16),
            pltpu.VMEM(((width + size) * height, tile), BF16),
            pltpu.VMEM(((width + 2 + size) * height, channels), F32),
            pltpu.VMEM(((width + size) * height, channels), F32),
            pltpu.VMEM((9, SUB, tile), F32),
            pltpu.VMEM((2, SUB, tile), F32),
            pltpu.VMEM((tile, channels), BF16),
            pltpu.VMEM((tile, channels), BF16),
        ],
        compiler_params=pltpu.CompilerParams(vmem_limit_bytes=VMEM_LIMIT),
        cost_estimate=cost(60),
        name="mlp_both",
    )(*whole, biases, taps, three, valid)


SEGMENT = 24
ROWS = 16
BLOCK = SEGMENT * ROWS
SLOTS = LANES // SEGMENT


def vmem_call(kernel, out_shape, scratch, microseconds, name, *operands, ties=()):
    kernel, tie_specs = tied(kernel, len(operands), ties)
    return pl.pallas_call(
        kernel,
        out_shape=out_shape,
        in_specs=[pl.BlockSpec(memory_space=pltpu.VMEM)] * len(operands) + tie_specs,
        out_specs=jax.tree.map(lambda _: pl.BlockSpec(memory_space=pltpu.VMEM), out_shape),
        scratch_shapes=scratch,
        compiler_params=pltpu.CompilerParams(vmem_limit_bytes=VMEM_LIMIT),
        cost_estimate=cost(microseconds),
        name=name,
    )(*operands, *ties)


def lane_index():
    return lax.broadcasted_iota(jnp.int32, (SUB, LANES), 1)


def choose(mask, first, second):
    rows = first.shape[0]
    pair = [v.reshape(rows // SUB, SUB, LANES) for v in (first, second)]
    return jnp.where(mask[None], *pair).reshape(rows, LANES)


def tile_of(index):
    return slice(index * LANES, (index + 1) * LANES)


def pack_kernel(device_of, centre, x_ref, swap_ref, out_ref, mean_ref, square_ref, y, last):
    chans, rows, columns = x_ref.shape
    count = rows * columns
    for i in range(chans // SUB):
        part = slice(i * SUB, (i + 1) * SUB)
        values = x_ref[part]
        if centre:
            mean = jnp.sum(values, axis=(1, 2), keepdims=True) * (1.0 / count)
            values = values - mean
            square = jnp.sum(values * values, axis=(1, 2), keepdims=True)
            mean_ref[part] = jnp.broadcast_to(mean, (SUB, 1, LANES))
            square_ref[part] = jnp.broadcast_to(square, (SUB, 1, LANES))
        swapped = dot_nn(swap_ref[...], lower(values).reshape(SUB * rows, columns))
        y[:, part, :] = swapped.reshape(rows, SUB, columns)
    for t in range(columns // LANES):
        for tile in range(3):
            last[tile, :, tile_of(t)] = pltpu.roll(
                y[rows - 1, :, tile_of(t)], LANES - SUB * (tile + 1), 1
            )
        for r in range(rows - 1):
            if r % SLOTS:
                y[r, :, tile_of(t)] = pltpu.roll(y[r, :, tile_of(t)], SEGMENT * (r % SLOTS), 1)
    for s, device in enumerate(device_of):
        t, start = divmod(s * SEGMENT, LANES)
        place = (lane_index() - start) & (LANES - 1)
        over = LANES - start
        for tile in range(3):
            pieces = []
            for m in range(SLOTS):
                piece = y[tile * SLOTS + m, :, tile_of(t)]
                if over < SEGMENT:
                    beyond = y[tile * SLOTS + m, :, tile_of(t + 1)]
                    piece = choose(place - SEGMENT * m >= over, beyond, piece)
                pieces.append(piece)
            value = pieces[-1]
            for m in range(SLOTS - 2, -1, -1):
                value = choose(place < SEGMENT * (m + 1), pieces[m], value)
            source = t if start + SUB * tile < LANES else t + 1
            value = choose(place >= SEGMENT * SLOTS, last[tile, :, tile_of(source)], value)
            out_ref[device, :, tile_of(tile)] = lower(value)


def drop_stats(kernel, x_ref, swap_ref, out_ref, y, last):
    kernel(x_ref, swap_ref, out_ref, None, None, y, last)


def unpack_kernel(device_of, affine, got_ref, swap_ref, part_ref, base_ref, *rest):
    if affine:
        x_ref, coef_ref, out_ref, flat, y = rest
    else:
        out_ref, flat, y = rest
    chans, rows, columns = out_ref.shape
    flat[...] = got_ref[...].astype(F32)
    for t in range(columns // LANES):
        strips = []
        for s, device in enumerate(device_of):
            end = (s + 1) * SEGMENT - t * LANES
            if end > 0 and s * SEGMENT - t * LANES < LANES:
                strips.append((end, device))

        def pick(place, tile, strips=strips):
            value = flat[strips[-1][1], :, tile_of(tile)]
            for end, device in strips[-2::-1]:
                value = choose(place < end, flat[device, :, tile_of(tile)], value)
            return value

        for m in range(SLOTS):
            place = (lane_index() - SEGMENT * m) & (LANES - 1)
            for tile in range(3):
                value = pick(place, tile)
                if m:
                    value = pltpu.roll(value, LANES - SEGMENT * m, 1)
                y[tile * SLOTS + m, :, tile_of(t)] = value
        pieces = []
        for tile in range(3):
            place = (lane_index() + SUB * (tile + 1)) & (LANES - 1)
            pieces.append(pltpu.roll(pick(place, tile), SUB * (tile + 1), 1))
        part = part_ref[t]
        value = choose(part == 0, pieces[0], choose(part == 1, pieces[1], pieces[2]))
        y[rows - 1, :, tile_of(t)] = value
    for i in range(chans // SUB):
        part = slice(i * SUB, (i + 1) * SUB)
        mixed = lower(y[:, part, :]).reshape(SUB * rows, columns)
        value = dot_nn(swap_ref[...], mixed).reshape(SUB, rows, columns)
        if affine:
            for t in range(columns // LANES):
                lanes = tile_of(t)
                out_ref[part, :, lanes] = (
                    base_ref[part, :, lanes]
                    + value[:, :, lanes]
                    - coef_ref[0, part]
                    - coef_ref[1, part] * (x_ref[part, :, lanes] - coef_ref[2, part])
                )
        else:
            out_ref[part] = base_ref[part] + value


def first_kernel(
    got_ref,
    order_ref,
    offset_ref,
    vector_ref,
    weight_ref,
    unit_ref,
    g_ref,
    slope_ref,
    low_ref,
    *edge_refs,
):
    values = dot_nt(order_ref[...], got_ref[...])
    unit = values * vector_ref[0:1, :] + offset_ref[...]
    normed = unit * vector_ref[1:2, :] + vector_ref[2:3, :]
    first = dot_nt(lower(normed), weight_ref[...]) + vector_ref[3:4, :]
    active, slope = gelu_parts(first)
    shape = unit_ref.shape
    unit_ref[...] = unit.reshape(shape)
    g_ref[...] = active.reshape(shape)
    slope_ref[...] = slope.reshape(shape)
    low_ref[...] = lower(active).reshape(shape)
    put_edges(active, shape, *edge_refs)


def finish_kernel(
    shrink,
    up_rate,
    early_ref,
    last_ref,
    up_momentum,
    down_rows,
    first_momentum,
    second_momentum,
    third_momentum,
    up_weight,
    down_weight,
    square_weights,
    new_up,
    new_down,
    new_squares,
):
    new_up[...] = shrink * up_weight[...] - up_rate * dot_nn(
        lower(up_momentum[...]), early_ref[0]
    )
    new_down[...] = shrink * down_weight[...] - MATRIX_RATE * dot_nt(
        early_ref[1], lower(down_rows[...])
    )
    first = dot_split(split_low(first_momentum[...]), split_low(last_ref[...]))
    second = dot_nn(lower(second_momentum[...]), early_ref[2])
    third = dot_nn(lower(third_momentum[...]), early_ref[3])
    for k, ortho in enumerate((first, second, third)):
        new_squares[k] = shrink * square_weights[k] - MATRIX_RATE * ortho


class Strips:
    def __init__(self, local_chans, local_rows, columns):
        self.dp = lax.axis_size("dp")
        self.chan = lax.axis_size("chan")
        self.count = self.dp * self.chan
        self.local_chans = local_chans
        self.local_rows = local_rows
        self.columns = columns
        self.width = columns // self.count
        self.height = local_rows * self.dp
        self.channels = local_chans * self.chan
        self.device_of = []
        for d in range(self.dp):
            line = list(range(d * self.chan, (d + 1) * self.chan))
            self.device_of += line if d % 2 == 0 else line[::-1]
        d = lax.axis_index("dp")
        c = lax.axis_index("chan")
        self.index = d * self.chan + jnp.where(d % 2 == 0, c, self.chan - 1 - c)
        self.steps = self.height // ROWS
        self.fast = (
            self.width == SEGMENT
            and local_rows == ROWS
            and local_chans % SUB == 0
            and columns % LANES == 0
        )
        if self.fast:
            self.prepare()

    def prepare(self):
        mixed = np.arange(SUB * ROWS)
        swap = np.zeros((SUB * ROWS, SUB * ROWS), np.float32)
        swap[mixed, (mixed % SUB) * ROWS + mixed // SUB] = 1.0
        self.swap = jnp.asarray(swap, BF16)
        self.swap_back = jnp.asarray(swap.T, BF16)
        part = (np.arange(self.columns) % SEGMENT) // SUB
        part = part.reshape(-1, 1, LANES).astype(np.int32)
        self.part = jnp.asarray(np.broadcast_to(part, (part.shape[0], SUB, LANES)))
        start = (self.index * SEGMENT) % LANES
        w, r = np.divmod(np.arange(BLOCK), ROWS)
        last = r == ROWS - 1
        tile = np.where(last, w // SUB, r // SLOTS)
        shift = np.where(last, w % SUB - SUB, SEGMENT * (r % SLOTS) + w)
        lane = LANES * jnp.asarray(tile) + (start + jnp.asarray(shift)) % LANES
        self.order = (lane[:, None] == jnp.arange(BLOCK)[None, :]).astype(BF16)

    def pack(self, values, centre, ties=()):
        chans, rows, columns = values.shape
        blocks = jax.ShapeDtypeStruct((self.count, chans, BLOCK), BF16)
        stat = jax.ShapeDtypeStruct((chans, 1, LANES), F32)
        scratch = [pltpu.VMEM((rows, chans, columns), F32), pltpu.VMEM((3, chans, columns), F32)]
        kernel = functools.partial(pack_kernel, self.device_of, centre)
        if not centre:
            kernel = functools.partial(drop_stats, kernel)
            out = [blocks]
        else:
            out = [blocks, stat, stat]
        return vmem_call(kernel, out, scratch, 4, "pack", values, self.swap, ties=ties)

    def unpack(self, got, base, *affine, ties=()):
        scratch = [pltpu.VMEM(got.shape, F32), pltpu.VMEM((ROWS,) + base.shape[:1] + base.shape[2:], F32)]
        kernel = functools.partial(unpack_kernel, self.device_of, bool(affine))
        return vmem_call(
            kernel,
            jax.ShapeDtypeStruct(base.shape, F32),
            scratch,
            5,
            "unpack",
            got,
            self.swap_back,
            self.part,
            base,
            *affine,
            ties=ties,
        )

    def move(self, blocks):
        return lax.all_to_all(blocks, BOTH, split_axis=0, concat_axis=0, tiled=True)

    def stage(self, kernel, inputs, outputs, microseconds, name, scratch=(), ties=()):
        kernel, tie_specs = tied(kernel, len(inputs), ties)

        def spec(value):
            shape = value.shape
            if len(shape) == 3 and shape[1:] == (self.height, self.channels):
                return pl.BlockSpec((shape[0], ROWS, shape[2]), lambda d: (0, d, 0))
            if len(shape) == 3 and shape[0] == self.steps:
                return pl.BlockSpec((None,) + shape[1:], lambda d: (d, 0, 0))
            return whole_spec(shape)

        return pl.pallas_call(
            kernel,
            grid=(self.steps,),
            in_specs=[spec(v) for v in inputs] + tie_specs,
            out_specs=jax.tree.map(spec, outputs),
            out_shape=outputs,
            scratch_shapes=scratch,
            compiler_params=pltpu.CompilerParams(vmem_limit_bytes=VMEM_LIMIT),
            cost_estimate=cost(microseconds),
            name=name,
        )(*inputs, *ties)

    def strips(self, dtype, columns=None):
        return jax.ShapeDtypeStruct((columns or self.width, self.height, self.channels), dtype)

    def edge_shapes(self, reach):
        return [self.strips(BF16, reach)] * 2 if reach <= self.width else []

    def blocks(self):
        return jax.ShapeDtypeStruct((self.steps, self.channels, BLOCK), BF16)

    def per_step(self, got):
        return got.reshape(self.steps, self.channels, BLOCK)

    def sums(self, rows):
        return jax.ShapeDtypeStruct((rows, self.channels), F32)

    def first_stage(self, got, offset, vectors, weight, ties):
        inputs = [self.per_step(got), self.order, offset[:, None, :], vectors, weight]
        outputs = [self.strips(F32)] * 3 + [self.strips(BF16)] + self.edge_shapes(11)
        unit, active, slope, low, *edges = self.stage(
            first_kernel, inputs, outputs, 7, "first_stage", ties=ties
        )
        return unit, active, slope, low, edges

    def leave(self):
        if self.fast:
            return [self.order], self.blocks()
        return [], self.strips(BF16)

    def reorder(self, blocks):
        lines = blocks.reshape((self.dp, self.chan) + blocks.shape[1:])
        lines = [lines[d] if d % 2 == 0 else lines[d][::-1] for d in range(self.dp)]
        return jnp.concatenate(lines, axis=0)

    def exchange(self, blocks):
        size = math.prod(blocks.shape[1:])
        shape = blocks.shape
        flat = (size // LANES, LANES) if size % LANES == 0 else (size,)
        moved = lax.all_to_all(
            blocks.reshape((self.count,) + flat), BOTH, split_axis=0, concat_axis=0, tiled=True
        )
        return moved.reshape(shape)

    def to_strips(self, values):
        blocks = values.reshape(self.local_chans, self.local_rows, self.count, self.width)
        blocks = self.reorder(jnp.transpose(blocks, (2, 0, 1, 3)))
        got = self.exchange(blocks)
        got = got.reshape(self.dp, self.chan, self.local_chans, self.local_rows, self.width)
        got = jnp.transpose(got, (4, 0, 3, 1, 2))
        return got.reshape(self.width, self.height, self.channels)

    def from_strips(self, values):
        blocks = values.reshape(self.width, self.dp, self.local_rows, self.chan, self.local_chans)
        blocks = jnp.transpose(blocks, (1, 3, 4, 2, 0))
        blocks = blocks.reshape(self.count, self.local_chans, self.local_rows, self.width)
        got = self.reorder(self.exchange(blocks))
        got = jnp.transpose(got, (1, 2, 0, 3))
        return got.reshape(self.local_chans, self.local_rows, self.columns)

    def halo(self, values, reach, edges=()):
        steps = -(-reach // self.width)
        left, right = [], []
        for step in range(1, steps + 1):
            take = min(self.width, reach - (step - 1) * self.width)
            forth = [
                (self.device_of[s], self.device_of[s + step]) for s in range(self.count - step)
            ]
            low, high = edges or (values[:take], values[self.width - take :])
            left.insert(0, lax.ppermute(high, BOTH, forth))
            right.append(lax.ppermute(low, BOTH, [(b, a) for a, b in forth]))
        if steps == 1:
            return left[0], values, right[0]
        return jnp.concatenate(left), values, jnp.concatenate(right)


def split_low(values):
    high = lower(values)
    return high, lower(values - high.astype(F32))


def dot_split(left, right):
    (left_high, left_low), (right_high, right_low) = left, right
    rows = left_high.shape[0]
    both = dot_nn(jnp.concatenate([left_high, left_low]), right_high)
    return both[:rows] + both[rows:] + dot_nn(left_high, right_low)


def factor_kernel(limit, rows_ref, factor_ref, gram, factor):
    size = gram.shape[0]
    eye = (
        lax.broadcasted_iota(jnp.int32, (size, size), 0)
        == lax.broadcasted_iota(jnp.int32, (size, size), 1)
    ).astype(F32)
    rows = rows_ref[...]
    if limit is not None:
        row = lax.broadcasted_iota(jnp.int32, rows.shape[1:], 0)
        rows = jnp.where((row < limit)[None], rows.astype(F32), 0.0).astype(BF16)
        rows = rows.reshape(-1, size)
    first = dot_tn(rows, rows)
    norm_value = jnp.sqrt(jnp.sum(first * eye, keepdims=True)) + 1e-07
    scale = 1.0 / norm_value
    gram[...] = first * (scale * scale)

    def polynomial_of(now, pair):
        square = dot_split(pair, pair)
        return square, ORDER_ONE * eye + ORDER_THREE * now + ORDER_FIVE * square

    def advance(step, carry):
        now = gram[...]
        pair = split_low(now)
        square, polynomial = polynomial_of(now, pair)
        cube = dot_split(pair, split_low(square))
        half = ORDER_ONE * now + ORDER_THREE * square + ORDER_FIVE * cube
        old = jnp.where(step == 0, eye * scale, factor[...])
        product = dot_split(split_low(jnp.concatenate([half, old])), split_low(polynomial))
        gram[...] = product[:size]
        factor[...] = product[size:]
        return carry

    factor[...] = eye
    lax.fori_loop(0, SCHULZ_STEPS - 1, advance, 0)
    now = gram[...]
    _, polynomial = polynomial_of(now, split_low(now))
    factor_ref[...] = dot_split(split_low(factor[...]), split_low(polynomial))


def orthogonal_factor(rows, ties=(), limit=None):
    size = rows.shape[-1]
    kernel, tie_specs = tied(functools.partial(factor_kernel, limit), 1, ties)
    return pl.pallas_call(
        kernel,
        out_shape=jax.ShapeDtypeStruct((size, size), F32),
        in_specs=[pl.BlockSpec(memory_space=pltpu.VMEM)] + tie_specs,
        out_specs=pl.BlockSpec(memory_space=pltpu.VMEM),
        scratch_shapes=[pltpu.VMEM((size, size), F32), pltpu.VMEM((size, size), F32)],
        compiler_params=pltpu.CompilerParams(vmem_limit_bytes=VMEM_LIMIT),
        cost_estimate=cost(13),
        name="orthogonal_factor",
    )(rows, *ties)


def behind(values, *earlier):
    any_spec = pl.BlockSpec(memory_space=pl.ANY)
    return pl.pallas_call(
        lambda *refs: None,
        out_shape=jax.ShapeDtypeStruct(values.shape, values.dtype),
        in_specs=[any_spec] * (1 + len(earlier)),
        out_specs=any_spec,
        input_output_aliases={0: 0},
        cost_estimate=cost(0.1),
        name="behind",
    )(values, *earlier)


def share(values, axes):
    count = lax.axis_size(axes)
    copies = jnp.broadcast_to(values[None], (count,) + values.shape)
    return lax.all_to_all(copies, axes, split_axis=0, concat_axis=0, tiled=True)


def exchange(values, axis):
    return lax.all_to_all(values, axis, split_axis=0, concat_axis=0, tiled=True)


def turns(values, axis):
    count = lax.axis_size(axis)
    return [
        lax.ppermute(values, axis, [(i, (i + r) % count) for i in range(count)])
        for r in range(count - 1, 0, -1)
    ] + [values]


def share_by_turns(values, axis):
    count = lax.axis_size(axis)
    if count > 8:
        return lax.all_gather(values, axis)
    got = turns(values, axis)
    start = count - 1 - lax.axis_index(axis)
    return lax.dynamic_slice_in_dim(jnp.stack(got + got), start, count, axis=0)


def share_dp(values):
    return share_by_turns(values, "dp")


def scatter_dp(blocks):
    count = lax.axis_size("dp")
    here = lax.axis_index("dp")

    def block(step):
        return lax.dynamic_index_in_dim(blocks, (here + step) % count, axis=0, keepdims=False)

    result = block(0).astype(F32)
    for step in range(1, count):
        pairs = [(i, (i + step) % count) for i in range(count)]
        result = result + lax.ppermute(block(step), "dp", pairs).astype(F32)
    return result


def share_rows(rows):
    chan = lax.axis_size("chan")
    count = rows.shape[0]
    if chan > 8 or count % (4 * SUB):
        return share(rows, "chan").reshape(-1, rows.shape[1])
    half = count // 2
    parity = lax.axis_index("chan") % 2
    across = [(i, i ^ 1) for i in range(chan)]
    kept = lax.dynamic_slice_in_dim(rows, parity * half, half, axis=0)
    sent = lax.dynamic_slice_in_dim(rows, (1 - parity) * half, half, axis=0)
    held = jnp.concatenate([kept, lax.ppermute(sent, "chan", across)])
    held = jnp.concatenate(
        [held]
        + [
            lax.ppermute(held, "chan", [(i, (i + 2 * step) % chan) for i in range(chan)])
            for step in range(1, chan // 2)
        ]
    )
    return jnp.concatenate([held, lax.ppermute(held, "chan", across)])


def for_dp(parts):
    dp = lax.axis_size("dp")
    blocks = []
    for part in parts:
        chan, rows, lanes = part.shape
        each = -(-rows // (SUB * dp)) * SUB
        part = jnp.pad(part, ((0, 0), (0, each * dp - rows), (0, 0)))
        blocks.append(part.reshape(chan, dp, each, lanes))
    return jnp.concatenate(blocks, axis=2)


def scattered(blocks, *earlier):
    chan, dp, rows, lanes = blocks.shape
    parity = lax.axis_index("chan") % 2
    blocks = blocks.reshape(chan // 2, 2, dp, rows, lanes)
    kept = lax.dynamic_index_in_dim(blocks, parity, axis=1, keepdims=False)
    sent = lax.dynamic_index_in_dim(blocks, 1 - parity, axis=1, keepdims=False)
    got = behind(lax.ppermute(sent, "chan", [(i, i ^ 1) for i in range(chan)]), *earlier)
    both = lower(kept.astype(F32) + got.astype(F32))
    return lower(scatter_dp(jnp.transpose(both, (1, 0, 2, 3))))


def summed_over_chan(blocks, *earlier):
    half = blocks.shape[0]
    place = lax.axis_index("chan") // 2

    def block(step):
        return lax.dynamic_index_in_dim(blocks, (place + step) % half, axis=0, keepdims=False)

    result = block(0).astype(F32)
    for step in range(1, half):
        pairs = [(i, (i + 2 * step) % (2 * half)) for i in range(2 * half)]
        got = lax.ppermute(block(step), "chan", pairs)
        if step == 1:
            got = behind(got, *earlier)
        result = result + got.astype(F32)
    return lower(result)


def own_rows(rows, counts):
    dp = lax.axis_size("dp")
    got = share_dp(rows).astype(F32)
    out, place = [], 0
    for count in counts:
        each = -(-count // (SUB * dp)) * SUB
        out.append(got[:, place : place + each].reshape(dp * each, -1)[:count])
        place += each
    return out


def body(
    block_input,
    cotangent,
    canvas_rows,
    square_weights,
    square_momenta,
    up_weight,
    up_momentum,
    down_weight,
    down_momentum,
    narrow_vectors,
    narrow_momenta,
    wide_vectors,
    wide_momenta,
    lka_kernels,
    lka_momenta,
    mlp_kernel,
    mlp_momentum,
):
    local_chans, local_rows, columns = block_input.shape
    hidden_local = up_weight.shape[0]
    grid = Strips(local_chans, local_rows, columns)
    width, height, channels = grid.width, grid.height, grid.channels
    hidden = hidden_local * grid.chan
    own = width * height
    pixel_count = height * columns
    local_count = local_rows * columns
    here = lax.axis_index("chan")


    if grid.fast:
        blocks, local_mean, local_square = grid.pack(block_input, True)
        local_mean, local_square = local_mean[:, 0, 0], local_square[:, 0, 0]
        sent_x = grid.move(blocks)
    else:
        local_mean = jnp.sum(block_input, axis=(1, 2)) / local_count
        centred = block_input - local_mean[:, None, None]
        local_square = jnp.sum(centred * centred, axis=(1, 2))
        sent_x = grid.to_strips(lower(centred))
    stats = share_dp(jnp.stack([local_mean, local_square]))
    own_mean = jnp.mean(stats[:, 0], axis=0)
    apart = stats[:, 0] - own_mean
    variance = (jnp.sum(stats[:, 1], axis=0) + local_count * jnp.sum(apart * apart, axis=0)) / (
        pixel_count
    )
    own_rstd = lax.rsqrt(variance + EPSILON)

    fold = hidden_local // local_chans
    vectors = jnp.concatenate(
        [
            own_rstd[:, None],
            (apart * own_rstd).T,
            narrow_vectors.T,
            lka_kernels,
            jnp.transpose(wide_vectors.reshape(2, fold, local_chans), (2, 0, 1)).reshape(
                local_chans, -1
            ),
            jnp.transpose(mlp_kernel.reshape(fold, local_chans, 9), (1, 2, 0)).reshape(
                local_chans, -1
            ),
        ],
        axis=1,
    )
    count = vectors.shape[1]
    high = lax.reduce_precision(vectors, exponent_bits=8, mantissa_bits=7)
    vectors = lower(jnp.concatenate([high, vectors - high], axis=1))
    vectors = jnp.pad(vectors, ((0, 0), (0, channels - 2 * count)))
    packed = lax.all_gather(
        jnp.concatenate([lower(square_weights).reshape(3 * local_chans, channels), vectors]), "chan"
    )
    low_one, low_two, low_three = (
        packed[:, k * local_chans : (k + 1) * local_chans].reshape(channels, channels)
        for k in range(3)
    )
    vectors = packed[:, 3 * local_chans : 4 * local_chans].astype(F32)
    vectors = vectors[:, :, :count] + vectors[:, :, count : 2 * count]
    vectors = vectors.reshape(channels, count).T
    rstd_one, spread = vectors[0], vectors[1 : 1 + grid.dp]
    vectors = vectors[1 + grid.dp :]
    narrow, lka_taps = vectors[:12], vectors[12:86]
    hidden_rows = vectors[86:].reshape(11, fold, grid.chan, local_chans)
    hidden_rows = jnp.transpose(hidden_rows, (0, 2, 1, 3)).reshape(11, hidden)
    wide, mlp_taps = hidden_rows[:2], hidden_rows[2:]

    if grid.fast:
        unit_one, gated_in, first_slope, gated_low, edges = grid.first_stage(
            sent_x,
            spread,
            jnp.concatenate([rstd_one[None], narrow[:3]]),
            low_one,
            (),
        )
    else:
        offset = jnp.repeat(spread, local_rows, axis=0)
        unit_one = sent_x.astype(F32) * rstd_one + offset
        low_normed = lower(unit_one * narrow[0] + narrow[1]).reshape(own, channels)
        first = dot_nt(low_normed, low_one) + narrow[2]
        gated_in, first_slope = (v.reshape(unit_one.shape) for v in gelu_parts(first))
        gated_low = lower(gated_in)
        edges = ()
    g_parts = grid.halo(gated_low, 11, edges)

    masks_five, masks_seven, masks_three, valid = make_masks(
        canvas_rows, grid.index, height, columns, width, [gated_low]
    )

    if grid.fast:
        cot_blocks = grid.pack(cotangent, False, [gated_low])[0]
        cot_got = grid.move(behind(cot_blocks, g_parts[0], g_parts[2]))
    t5_ext, after_seven = attention_forward(
        g_parts, lka_taps, narrow[3:5], masks_five, masks_seven, valid
    )
    pair = jnp.concatenate([lower(up_weight), lower(down_weight.T)])
    if grid.fast:
        pair = behind(pair, cot_got, after_seven)
    pair = lax.all_gather(pair, "chan")
    if hidden_local % (4 * SUB):
        pair = [pair[:, :hidden_local], pair[:, hidden_local:]]
        pair = jnp.concatenate([v.reshape(hidden, channels) for v in pair])[None]
    if grid.fast:
        leaving = [grid.per_step(cot_got), grid.order]
        unpacked = [grid.strips(BF16)]
    else:
        cot = grid.to_strips(lower(cotangent))
        leaving, unpacked = [cot], []
    q, gated, branch_one, middle, totals, low_edge, high_edge, *unpacked = grid.stage(
        functools.partial(middle_kernel, grid.fast),
        [
            after_seven,
            gated_in,
            unit_one,
            jnp.concatenate([(1.0 / rstd_one)[None], narrow[:2], narrow[5:8]]),
            low_two,
            low_three,
            *leaving,
        ],
        [grid.strips(F32), grid.strips(BF16), grid.strips(F32), grid.strips(F32)]
        + [jax.ShapeDtypeStruct((grid.count, 2, channels), F32)]
        + [grid.strips(BF16, 3)] * 2
        + unpacked,
        8,
        "middle_stage",
    )
    cot = unpacked[0] if grid.fast else cot

    totals = exchange(totals, BOTH)
    mid_parts = grid.halo(middle, 3, (low_edge, high_edge))
    ff, back_norm, up_part, down_part, norm_sums = mlp_both(
        mid_parts,
        cot,
        totals,
        narrow,
        pair,
        wide,
        mlp_taps,
        masks_three,
        valid,
    )
    extra, leaving = grid.leave()
    out_part, out_sums = grid.stage(
        output_kernel,
        [
            ff.reshape(unit_one.shape),
            branch_one,
            cot,
            jnp.stack([narrow[7], narrow[10], narrow[11]]),
            *extra,
        ],
        [leaving, grid.sums(2)],
        5,
        "output_stage",
    )

    def rows_for(part, rows):
        return part.reshape(grid.chan, rows, -1)

    norm_sums = exchange(norm_sums, BOTH)

    norm_grad, back_gated, back_seven, weight_two, weight_three, branch_sums, *rest = grid.stage(
        functools.partial(branch_kernel, width >= 12),
        [
            back_norm.reshape(unit_one.shape),
            middle,
            cot,
            branch_one,
            gated,
            gated_in,
            after_seven,
            totals,
            norm_sums,
            narrow,
            low_two,
            low_three,
        ],
        [
            grid.strips(F32),
            grid.strips(F32),
            grid.strips(BF16),
            jax.ShapeDtypeStruct((channels, channels + SIDE_WIDTH), BF16),
            jax.ShapeDtypeStruct((channels, channels + SIDE_WIDTH), BF16),
            grid.sums(6),
        ]
        + grid.edge_shapes(12),
        8,
        "branch_stage",
        [pltpu.VMEM((channels, channels), F32)] * 2,
        [out_part],
    )
    d7_parts = grid.halo(back_seven, 12, rest)
    if grid.fast:
        out_blocks = out_part.reshape(grid.count, local_chans, BLOCK)
        out_got = grid.move(out_blocks)
    else:
        out_got = grid.from_strips(out_part)
        block_output = block_input + out_got.astype(F32)

    seven_part = tap_sums_seven(back_seven, t5_ext, masks_seven, ())
    back_g, d5, bias_three = attention_backward(
        d7_parts, lka_taps, masks_five, masks_seven, valid, [seven_part]
    )
    dp_sums = scattered(
        for_dp(
            [
                rows_for(up_part, hidden_local),
                rows_for(down_part, hidden_local),
                jnp.concatenate(
                    [rows_for(weight_two, local_chans), rows_for(weight_three, local_chans)], axis=1
                ),
            ]
        ),
        seven_part,
    )
    five_part = tap_sums_five(d5, g_parts, masks_five, [out_got])
    extra, leaving = grid.leave()
    each = -(-local_chans // grid.dp)
    few = -(-86 // grid.count)
    row_count = -(-(each + few) // (2 * SUB)) * (2 * SUB)
    in_part, last_rows = grid.stage(
        functools.partial(last_kernel, (grid.dp, grid.chan, local_chans, each, few)),
        [
            back_g,
            back_gated,
            q,
            first_slope,
            unit_one,
            norm_grad,
            cot,
            narrow,
            rstd_one[None],
            low_one,
            out_sums,
            branch_sums,
            bias_three,
            five_part,
            seven_part,
            *extra,
        ],
        [leaving, jax.ShapeDtypeStruct((grid.count, row_count, channels), BF16)],
        7,
        "last_stage",
        [
            pltpu.VMEM((channels, channels), F32),
            pltpu.VMEM((SUB, channels), F32),
            pltpu.VMEM((grid.count * few, channels), F32),
            pltpu.VMEM((grid.count, row_count, channels), F32),
        ],
    )
    chan_sums = summed_over_chan(behind(dp_sums, bias_three), last_rows)
    grads = own_rows(chan_sums, [hidden_local, hidden_local, 2 * local_chans])
    up_grad, side_grad = grads[0][:, :channels], grads[0][:, channels : channels + 11]
    down_grad = grads[1][:, :channels]
    second_grad = grads[2][:local_chans, :channels]
    third_grad = grads[2][local_chans:, :channels]
    second_momentum = MATRIX_MOMENTUM * square_momenta[1] + second_grad
    third_momentum = MATRIX_MOMENTUM * square_momenta[2] + third_grad
    new_up_momentum = MATRIX_MOMENTUM * up_momentum + up_grad
    down_rows = MATRIX_MOMENTUM * down_momentum.T + down_grad

    tall = [new_up_momentum, down_rows, second_momentum, third_momentum]
    tall = [jnp.pad(lower(v), ((0, hidden_local - v.shape[0]), (0, 0))) for v in tall]
    mine_of_four = lax.dynamic_index_in_dim(
        jnp.stack(tall), jnp.minimum(lax.axis_index("dp"), len(tall) - 1), keepdims=False
    )
    if grid.fast:
        block_output = grid.unpack(out_got, block_input, ties=[last_rows])

    summed = jnp.sum(exchange(last_rows, BOTH).astype(F32), axis=0)
    old_first = jnp.pad(square_momenta[0], ((0, each * grid.dp - local_chans), (0, 0)))
    old_first = lax.dynamic_slice_in_dim(old_first, lax.axis_index("dp") * each, each, axis=0)
    old_first = jnp.pad(MATRIX_MOMENTUM * old_first, ((0, row_count - each), (0, 0)))
    shared = share(lower(summed + old_first), BOTH)

    own_factor = orthogonal_factor(share_rows(mine_of_four))
    early_factor = share_dp(behind(lower(own_factor), shared))
    last_factor = orthogonal_factor(shared, [early_factor], each)
    if grid.fast:
        in_part = in_part.reshape(grid.count, local_chans, BLOCK)
        in_part = grid.move(behind(in_part, shared))
    else:
        in_part = grid.from_strips(in_part).astype(F32)
    own_first = shared[:, :each].reshape(grid.dp, grid.chan, each, channels)
    own_first = lax.dynamic_index_in_dim(own_first, here, axis=1, keepdims=False)
    own_first = own_first.reshape(-1, channels)[:local_chans].astype(F32)
    last_sums = shared[:, each : each + few].reshape(-1, channels).astype(F32)

    def mine(rows, size):
        return lax.dynamic_slice_in_dim(rows, here * size, size, axis=-1)

    narrow_grad = mine(
        jnp.concatenate([last_sums[:8], branch_sums[5:6], branch_sums[4:5], last_sums[10:12]]),
        local_chans,
    )
    own_gain = narrow_vectors[0]
    slope_here = own_rstd * own_rstd * own_gain * narrow_grad[0] / pixel_count
    level_here = own_rstd * own_gain * narrow_grad[1] / pixel_count
    if grid.fast:
        coefs = jnp.stack([level_here, slope_here, own_mean])
        coefs = jnp.broadcast_to(coefs[:, :, None, None], coefs.shape + (1, LANES))
        input_grad = grid.unpack(in_part, cotangent, block_input, coefs)
    else:
        input_grad = (
            cotangent
            + in_part
            - level_here[:, None, None]
            - slope_here[:, None, None] * (block_input - own_mean[:, None, None])
        )

    new_square_momenta = jnp.stack([own_first, second_momentum, third_momentum])
    new_up_weight, new_down_weight, new_square_weights = vmem_call(
        functools.partial(
            finish_kernel,
            1.0 - MATRIX_RATE * WEIGHT_DECAY,
            MATRIX_RATE * math.sqrt(max(1.0, HID / C)),
        ),
        [
            jax.ShapeDtypeStruct(v.shape, F32) for v in (up_weight, down_weight, square_weights)
        ],
        [],
        4,
        "finish",
        early_factor,
        last_factor,
        new_up_momentum,
        down_rows,
        own_first,
        second_momentum,
        third_momentum,
        up_weight,
        down_weight,
        square_weights,
    )

    lka_grad = mine(last_sums[12:86], local_chans).T
    wide_grad, mlp_grad = side_grad[:, :2].T, side_grad[:, 2:]
    vector_step = VECTOR_RATE / math.sqrt(pixel_count)
    new_narrow_momenta = VECTOR_MOMENTUM * narrow_momenta + narrow_grad
    new_narrow_vectors = narrow_vectors - vector_step * new_narrow_momenta
    new_wide_momenta = VECTOR_MOMENTUM * wide_momenta + wide_grad
    new_wide_vectors = wide_vectors - vector_step * new_wide_momenta
    new_lka_momenta = VECTOR_MOMENTUM * lka_momenta + lka_grad
    new_lka_kernels = lka_kernels - vector_step * new_lka_momenta
    new_mlp_momentum = VECTOR_MOMENTUM * mlp_momentum + mlp_grad
    new_mlp_kernel = mlp_kernel - vector_step * new_mlp_momentum
    return (
        block_output,
        input_grad,
        new_square_weights,
        new_square_momenta,
        new_up_weight,
        new_up_momentum,
        new_down_weight,
        down_rows.T,
        new_narrow_vectors,
        new_narrow_momenta,
        new_wide_vectors,
        new_wide_momenta,
        new_lka_kernels,
        new_lka_momenta,
        new_mlp_kernel,
        new_mlp_momentum,
    )


def solution(mesh):
    placed = (
        P("chan", "dp", None),
        P("chan", "dp", None),
        P(),
        P(None, "chan", None),
        P(None, "chan", None),
        P("chan", None),
        P("chan", None),
        P(None, "chan"),
        P(None, "chan"),
        P(None, "chan"),
        P(None, "chan"),
        P(None, "chan"),
        P(None, "chan"),
        P("chan", None),
        P("chan", None),
        P("chan", None),
        P("chan", None),
    )
    return jax.shard_map(
        body,
        mesh=mesh,
        in_specs=placed,
        out_specs=(
            P("chan", "dp", None),
            P("chan", "dp", None),
            P(None, "chan", None),
            P(None, "chan", None),
            P("chan", None),
            P("chan", None),
            P(None, "chan"),
            P(None, "chan"),
            P(None, "chan"),
            P(None, "chan"),
            P(None, "chan"),
            P(None, "chan"),
            P("chan", None),
            P("chan", None),
            P("chan", None),
            P("chan", None),
        ),
        check_vma=False,
    )
```

```python
import functools
import math

import jax
import jax.numpy as jnp
import numpy as np
from jax import lax
from jax.experimental import pallas as pl
from jax.experimental.pallas import tpu as pltpu
from jax.sharding import PartitionSpec as P

C = 320
HID = 1280
SCHULZ_STEPS = 5
EPSILON = 1e-05
ORDER_ONE = 3.4445
ORDER_THREE = -4.775
ORDER_FIVE = 2.0315
MATRIX_MOMENTUM = 0.95
VECTOR_MOMENTUM = 0.9
MATRIX_RATE = 0.3
VECTOR_RATE = 0.2
WEIGHT_DECAY = 0.01
HIGHEST = lax.Precision.HIGHEST
BOTH = ("dp", "chan")
LANES = 128
SUB = 8
HIDDEN_TILE = 256
VMEM_LIMIT = 56 * 1024 * 1024
SIDE_WIDTH = 64
F32 = jnp.float32
BF16 = jnp.bfloat16


def lower(values):
    return values.astype(BF16)


def cost(microseconds):
    return pl.CostEstimate(
        flops=int(microseconds * 1e9), bytes_accessed=int(microseconds * 3e6), transcendentals=0
    )


def add_row(ref, row, values):
    ref[row : row + 1, :] = ref[row : row + 1, :] + jnp.sum(values, axis=0, keepdims=True)


def gelu_parts(values):
    cdf = 0.5 * (1.0 + lax.erf(values * 0.7071067811865476))
    slope = cdf + values * jnp.exp(-0.5 * values * values) * 0.3989422804014327
    return values * cdf, slope


def masks_kernel(columns, width, rows_ref, five_ref, seven_ref, three_ref, valid_ref):
    height = five_ref.shape[1]
    row = lax.broadcasted_iota(jnp.int32, (height, LANES), 0)

    def canvas(position):
        number = jnp.zeros((height, LANES), jnp.int32)
        end = 0
        for k in range(rows_ref.shape[0] - 1):
            end = end + rows_ref[k]
            number = number + jnp.where(position >= end, 1, 0)
        return number

    own = canvas(row)
    for ref, side, dilation in ((five_ref, 5, 1), (seven_ref, 7, 3), (three_ref, 3, 1)):
        for tap in range(side):
            other = row + (tap - side // 2) * dilation
            inside = (other >= 0) & (other < height) & (canvas(other) == own)
            ref[tap] = jnp.where(inside, 1.0, 0.0)
    count = valid_ref.shape[0]
    place = lax.broadcasted_iota(jnp.int32, (count, 1, LANES), 0) - (count - width) // 2
    place = place + rows_ref[rows_ref.shape[0] - 1] * width
    valid_ref[...] = jnp.where((place >= 0) & (place < columns), 1.0, 0.0)


def make_masks(canvas_rows, index, height, columns, width, ties):
    scalars = jnp.concatenate([canvas_rows, index[None].astype(jnp.int32)])
    kernel, tie_specs = tied(functools.partial(masks_kernel, columns, width), 1, ties)
    return pl.pallas_call(
        kernel,
        out_shape=[jax.ShapeDtypeStruct((k, height, LANES), F32) for k in (5, 7, 3)]
        + [jax.ShapeDtypeStruct((width + 18, 1, LANES), F32)],
        in_specs=[pl.BlockSpec(memory_space=pltpu.SMEM)] + tie_specs,
        out_specs=[pl.BlockSpec(memory_space=pltpu.VMEM)] * 4,
        cost_estimate=cost(1),
        name="masks",
    )(scalars, *ties)


def largest_divisor(number, most):
    for candidate in range(min(number, most), 0, -1):
        if number % candidate == 0:
            return candidate
    return 1


def roll_rows(values, shift):
    rows = values.shape[0]
    if shift % rows == 0:
        return values
    return pltpu.roll(values, shift % rows, 0)


def packed_rows(dtype):
    return SUB if dtype == F32 else 2 * SUB


def times_tap(tap, column):
    rows, lanes = column.shape
    each = packed_rows(column.dtype)
    return (tap[None] * column.reshape(rows // each, each, lanes)).reshape(rows, lanes)


def fold_rows(values):
    rows, lanes = values.shape
    each = packed_rows(values.dtype)
    values = values.reshape(rows // each, each, lanes)
    total = values[0]
    for k in range(1, rows // each):
        total = total + values[k]
    total = total.astype(F32)
    return total if each == SUB else total[:SUB] + total[SUB:]


def group_base(step, size, dilation):
    if dilation == 1:
        return step * size
    return (step // dilation) * (size * dilation) + step % dilation


UNROLL = 4


def run_groups(groups, step_body, carry):
    full = groups // UNROLL

    def chunk(index, carry):
        for u in range(UNROLL):
            carry = step_body(index * UNROLL + u, carry)
        return carry

    carry = lax.fori_loop(0, full, chunk, carry)
    for step in range(full * UNROLL, groups):
        carry = step_body(jnp.int32(step), carry)
    return carry


def conv_columns(load, tap, mask, side, dilation, columns, most, emit):
    size = largest_divisor(columns // dilation, most)

    def step_body(step, carry):
        base = group_base(step, size, dilation)
        totals = [None] * size
        for i in range(side):
            sums = [None] * size
            for c in range(size + side - 1):
                column = load(base + dilation * c)
                for j in range(side):
                    q = c - j
                    if 0 <= q < size:
                        term = times_tap(tap(i, j), column)
                        sums[q] = term if sums[q] is None else sums[q] + term
            offset = dilation * (i - side // 2)
            for q in range(size):
                term = sums[q].astype(F32)
                term = term if offset == 0 else mask(i) * roll_rows(term, -offset)
                totals[q] = term if totals[q] is None else totals[q] + term
        for q in range(size):
            emit(base + dilation * q, totals[q])
        return carry

    run_groups(columns // size, step_body, 0)


def tap_gradients(load_grad, load, mask, side, dilation, columns, most, store):
    size = largest_divisor(columns // dilation, most)
    lanes = LANES
    for i in range(side):
        offset = dilation * (i - side // 2)

        def step_body(step, sums, i=i, offset=offset):
            sums = list(sums)
            base = group_base(step, size, dilation)
            shifted = []
            for q in range(size):
                gradient = load_grad(base + dilation * q)
                if offset != 0:
                    moved = roll_rows(mask(i) * gradient.astype(F32), offset)
                    gradient = moved.astype(gradient.dtype)
                shifted.append(gradient)
            for c in range(size + side - 1):
                column = load(base + dilation * c)
                for j in range(side):
                    q = c - j
                    if 0 <= q < size:
                        sums[j] = sums[j] + fold_rows(shifted[q] * column)
            return tuple(sums)

        sums = run_groups(
            columns // size,
            step_body,
            tuple(jnp.zeros((SUB, lanes), F32) for _ in range(side)),
        )
        for j in range(side):
            store(i * side + j, jnp.sum(sums[j], axis=0, keepdims=True))


def spread_taps(kernel_ref, spread_ref, count):
    rows, lanes = spread_ref.shape[1:]
    for index in range(count):
        row = jnp.broadcast_to(kernel_ref[index : index + 1, :], (rows, lanes))
        spread_ref[index] = row.astype(spread_ref.dtype)


def join(target, pieces):
    place = 0
    for piece, first, count in pieces:
        target[place : place + count] = piece[first : first + count].astype(target.dtype)
        place += count


def attention_forward_kernel(
    width,
    left_ref,
    g_ref,
    right_ref,
    kernel_ref,
    bias_ref,
    five_ref,
    seven_ref,
    valid_ref,
    t5_ref,
    t7_ref,
    spread,
    gf,
):
    spread_taps(kernel_ref, spread, 74)
    join(gf, [(left_ref, 0, 11), (g_ref, 0, width), (right_ref, 0, 11)])
    bias_five = bias_ref[0:1, :]
    bias_seven = bias_ref[1:2, :]

    def emit_five(w, value):
        t5_ref[w] = lower((value + bias_five) * valid_ref[w])

    conv_columns(
        lambda w: gf[w],
        lambda i, j: spread[i * 5 + j],
        lambda i: five_ref[i],
        5,
        1,
        width + 18,
        3,
        emit_five,
    )

    def emit_seven(w, value):
        t7_ref[w] = lower(value + bias_seven)

    conv_columns(
        lambda w: t5_ref[w],
        lambda i, j: spread[25 + i * 7 + j],
        lambda i: seven_ref[i],
        7,
        3,
        width,
        2,
        emit_seven,
    )


def attention_backward_kernel(
    width,
    left_ref,
    d7_ref,
    right_ref,
    kernel_ref,
    five_ref,
    seven_ref,
    valid_ref,
    dg_ref,
    d5_ref,
    bias_ref,
    spread,
    d7,
    d5,
):
    spread_taps(kernel_ref, spread, 74)
    join(d7, [(left_ref, 0, 12), (d7_ref, 0, width), (right_ref, 0, 12)])

    def emit_five(w, value):
        d5[w] = lower(value * valid_ref[w + 6])

    conv_columns(
        lambda w: d7[w],
        lambda i, j: spread[25 + 48 - (i * 7 + j)],
        lambda i: seven_ref[i],
        7,
        3,
        width + 6,
        2,
        emit_five,
    )

    def emit_g(w, value):
        dg_ref[w] = value

    conv_columns(
        lambda w: d5[w + 1],
        lambda i, j: spread[24 - (i * 5 + j)],
        lambda i: five_ref[i],
        5,
        1,
        width,
        3,
        emit_g,
    )
    d5_ref[...] = d5[3 : 3 + width]
    sums = lax.fori_loop(
        0,
        width,
        lambda w, sums: sums + fold_rows(d5[w + 3].astype(F32)),
        jnp.zeros((SUB, LANES), F32),
    )
    bias_ref[0:1, :] = jnp.sum(sums, axis=0, keepdims=True)


def tap_seven_kernel(width, d7_ref, t5_ref, seven_ref, taps_ref):
    def store(index, value):
        taps_ref[index : index + 1, :] = value

    tap_gradients(
        lambda w: d7_ref[w], lambda w: t5_ref[w], lambda i: seven_ref[i], 7, 3, width, 2, store
    )


def tap_five_kernel(width, d5_ref, left_ref, g_ref, right_ref, five_ref, taps_ref, gf):
    join(gf, [(left_ref, 9, 2), (g_ref, 0, width), (right_ref, 0, 2)])

    def store(index, value):
        taps_ref[index : index + 1, :] = value

    tap_gradients(
        lambda w: d5_ref[w], lambda w: gf[w], lambda i: five_ref[i], 5, 1, width, 3, store
    )


def dot_nt(left, right):
    return lax.dot_general(left, right, (((1,), (1,)), ((), ())), preferred_element_type=F32)


def dot_nn(left, right):
    return lax.dot_general(left, right, (((1,), (0,)), ((), ())), preferred_element_type=F32)


def dot_tn(left, right):
    return lax.dot_general(left, right, (((0,), (0,)), ((), ())), preferred_element_type=F32)


def conv_three(load, tap, mask, size):
    totals = [None] * size
    for i in range(3):
        sums = [None] * size
        for c in range(size + 2):
            column = load(c)
            for j in range(3):
                q = c - j
                if 0 <= q < size:
                    term = times_tap(tap(i, j), column)
                    sums[q] = term if sums[q] is None else sums[q] + term
        for q in range(size):
            term = sums[q].astype(F32)
            term = term if i == 1 else mask(i) * roll_rows(term, 1 - i)
            totals[q] = term if totals[q] is None else totals[q] + term
    return totals


def mlp_kernel_body(
    width,
    height,
    mid_left,
    mid_ref,
    mid_right,
    cot_ref,
    totals_ref,
    vector_ref,
    pair_ref,
    bias_ref,
    kernel_ref,
    three_ref,
    valid_ref,
    ff_ref,
    dn2_ref,
    gup_ref,
    gdown_ref,
    sums_ref,
    spread,
    n2_ref,
    dff_ref,
    h,
    mixed,
    act,
    dh,
    ff,
    dn2,
    tap_acc,
    sum_acc,
    up_ref,
    downt_ref,
):
    tile, channels = up_ref.shape
    own = width * height
    step_id = pl.program_id(0)
    size = 2 if width % 2 == 0 else 1
    group = size * height
    parts = [slice(k * LANES, (k + 1) * LANES) for k in range(tile // LANES)]

    def rows_at(column, count=1):
        start = column * height
        if not isinstance(column, int):
            start = pl.multiple_of(start, height)
        return pl.ds(start, count * height)

    block = pair_ref.shape[1] // 2
    chunk = math.gcd(block, tile)
    for part in range(tile // chunk):
        row = step_id * tile + part * chunk
        place = lax.rem(row, block)
        here = slice(part * chunk, (part + 1) * chunk)
        for ref, start in ((up_ref, place), (downt_ref, place + block)):
            ref[here, :] = pair_ref[row // block, pl.ds(pl.multiple_of(start, chunk), chunk), :]
    spread_taps(kernel_ref, spread, 9)

    def second_statistics():
        totals = jnp.sum(totals_ref[...], axis=0) * (1.0 / (own * totals_ref.shape[0]))
        mean = totals[0:1, :]
        return mean, lax.rsqrt(totals[1:2, :] - mean * mean + EPSILON)

    @pl.when(step_id == 0)
    def _():
        mean, rstd = second_statistics()
        gain, shift, scale = vector_ref[8:9, :], vector_ref[9:10, :], vector_ref[11:12, :]

        def put_norm(column, values):
            unit = (values.astype(F32) - mean) * rstd
            n2_ref[rows_at(column), :] = lower(unit * gain + shift)

        def put_grad(column, values):
            dff_ref[rows_at(column), :] = lower(values.astype(F32) * scale)

        for w in range(2):
            put_norm(w, mid_left[w])
            put_norm(width + 2 + w, mid_right[w])
        put_grad(0, mid_left[2])
        put_grad(width + 1, mid_right[2])

        def own_column(w, carry):
            put_norm(w + 2, mid_ref[w])
            put_grad(w + 1, cot_ref[w])
            return carry

        lax.fori_loop(0, width, own_column, 0)
        n2_ref[rows_at(width + 4, size), :] = jnp.zeros((group, channels), BF16)
        act[0:group, :] = jnp.zeros((group, tile), BF16)
        dh[0:group, :] = jnp.zeros((group, tile), BF16)
        ff[...] = jnp.zeros_like(ff)
        dn2[...] = jnp.zeros_like(dn2)

    def expand(first, count):
        return dot_nt(n2_ref[rows_at(first, count), :], up_ref[...])

    def put_hidden(first, count, product):
        product = (product + bias_ref[0:1, :]).reshape(count, height, tile)
        for w in range(count):
            h[first + w] = lower(product[w] * valid_ref[first + w + 7, 0:1, 0:1])

    put_hidden(0, size + 2, expand(0, size + 2))

    def add_output(first):
        rows = rows_at(first, size)
        ff[rows, :] = ff[rows, :] + dot_nn(act[rows, :], downt_ref[...])

    def forward(step, carry):
        base = step * size
        ahead = expand(base + size + 2, size)
        back = dot_nt(dff_ref[rows_at(base, size), :], downt_ref[...])
        add_output(base)
        for lanes in parts:
            values = conv_three(
                lambda c: h[base + c, :, lanes],
                lambda i, j: spread[i * 3 + j, :, lanes],
                lambda i: three_ref[i],
                size,
            )
            for q in range(size):
                active, grade = gelu_parts(values[q] + bias_ref[1:2, lanes])
                act[rows_at(base + size + q), lanes] = lower(active)
                gradient = back[q * height : (q + 1) * height, lanes] * grade
                mixed[base + q, :, lanes] = lower(gradient * valid_ref[base + q + 8])
        put_hidden(base + size + 2, size, ahead)
        return carry

    groups = (width + 2) // size
    lax.fori_loop(0, groups, forward, 0)
    add_output(groups * size)
    tap_acc[...] = jnp.zeros_like(tap_acc)
    sum_acc[...] = jnp.zeros_like(sum_acc)

    def add_norm_grad(first):
        rows = rows_at(first, size)
        dn2[rows, :] = dn2[rows, :] + dot_nn(dh[rows, :], up_ref[...])

    def backward(step, carry):
        base = step * size
        add_norm_grad(base)
        for lanes in parts:
            values = conv_three(
                lambda c: mixed[base + c, :, lanes],
                lambda i, j: spread[8 - (i * 3 + j), :, lanes],
                lambda i: three_ref[i],
                size,
            )
            sums = [jnp.zeros((SUB, LANES), F32)] * 11
            shifted = []
            for q in range(size):
                low_value = lower(values[q])
                dh[rows_at(base + size + q), lanes] = low_value
                sums[9] = sums[9] + fold_rows(low_value.astype(F32))
                gradient = mixed[base + q + 1, :, lanes]
                wide_gradient = gradient.astype(F32)
                sums[10] = sums[10] + fold_rows(wide_gradient)
                moved = [lower(roll_rows(three_ref[i] * wide_gradient, i - 1)) for i in (0, 2)]
                shifted.append([moved[0], gradient, moved[1]])
            for c in range(size + 2):
                column = h[base + c + 1, :, lanes]
                for j in range(3):
                    q = c - j
                    if 0 <= q < size:
                        for i in range(3):
                            k = i * 3 + j
                            sums[k] = sums[k] + fold_rows(shifted[q][i] * column)
            for k in range(9):
                tap_acc[k, :, lanes] = tap_acc[k, :, lanes] + sums[k]
            for k in range(2):
                sum_acc[k, :, lanes] = sum_acc[k, :, lanes] + sums[9 + k]
        return carry

    lax.fori_loop(0, width // size, backward, 0)
    add_norm_grad(width)
    side = jnp.concatenate(
        [jnp.sum(sum_acc[...], axis=1), jnp.sum(tap_acc[...], axis=1), jnp.zeros((5, tile), F32)]
    )
    flip = (
        lax.broadcasted_iota(jnp.int32, (side.shape[0], SIDE_WIDTH), 0)
        == lax.broadcasted_iota(jnp.int32, (side.shape[0], SIDE_WIDTH), 1)
    ).astype(BF16)
    gup_ref[:, :channels] = lower(
        dot_tn(dh[group : group + own, :], n2_ref[2 * height : 2 * height + own, :])
    )
    gup_ref[:, channels:] = lower(dot_tn(lower(side), flip))
    first_own = group + height
    gdown_ref[:, :channels] = lower(
        dot_tn(act[first_own : first_own + own, :], dff_ref[height : height + own, :])
    )
    gdown_ref[:, channels:] = jnp.zeros((tile, SIDE_WIDTH), BF16)

    @pl.when(step_id == pl.num_programs(0) - 1)
    def _():
        mean, rstd = second_statistics()
        ff_ref[...] = ff[first_own : first_own + own, :]
        dn2_ref[...] = dn2[group : group + own, :]

        def column_sums(w, sums):
            rows = dn2[rows_at(w + size), :]
            unit = (mid_ref[w] - mean) * rstd
            shape = (height // SUB, SUB, channels)
            return (
                sums[0] + jnp.sum(rows.reshape(shape), axis=0),
                sums[1] + jnp.sum((rows * unit).reshape(shape), axis=0),
            )

        zero = jnp.zeros((SUB, channels), F32)
        sums = lax.fori_loop(0, width, column_sums, (zero, zero))
        sums = jnp.concatenate([jnp.sum(v, axis=0, keepdims=True) for v in sums])
        sums_ref[...] = jnp.broadcast_to(sums[None], sums_ref.shape)


def zero_first(*refs):
    @pl.when(pl.program_id(0) == 0)
    def _():
        for ref in refs:
            ref[...] = jnp.zeros_like(ref)


def flat(ref):
    return ref[...].reshape(ref.shape[0] * ref.shape[1], ref.shape[2])


def put_edges(values, shape, low_ref, high_ref):
    columns = lower(values).reshape(shape)
    reach = low_ref.shape[0]
    low_ref[...] = columns[:reach]
    high_ref[...] = columns[shape[0] - reach :]


def middle_kernel(
    unpack,
    t7_ref,
    g_ref,
    unit_ref,
    vector_ref,
    second_ref,
    third_ref,
    *rest,
):
    if unpack:
        got_ref, order_ref, q_ref, gq_ref, branch_ref, middle_ref, sums_ref, *rest = rest
        low_ref, high_ref, cot_ref = rest
        cot_ref[...] = lower(dot_nt(order_ref[...], got_ref[...])).reshape(cot_ref.shape)
    else:
        cot_ref, q_ref, gq_ref, branch_ref, middle_ref, sums_ref, low_ref, high_ref = rest
    zero_first(sums_ref)
    shape = unit_ref.shape
    row = lambda k: vector_ref[k : k + 1, :]
    attention = dot_nt(flat(t7_ref), second_ref[...]) + row(3)
    gated = lower(flat(g_ref) * attention)
    projected = dot_nt(gated, third_ref[...]) + row(4)
    unit = flat(unit_ref)
    branch = projected + (unit * row(1) + row(2))
    middle = unit * row(0) + row(5) * branch
    q_ref[...] = attention.reshape(shape)
    gq_ref[...] = gated.reshape(shape)
    branch_ref[...] = branch.reshape(shape)
    middle_ref[...] = middle.reshape(shape)
    columns = lower(middle).reshape(shape)
    low_ref[:2] = columns[:2]
    low_ref[2] = cot_ref[0]
    high_ref[:2] = columns[shape[0] - 2 :]
    high_ref[2] = cot_ref[shape[0] - 1]
    sums = [jnp.sum(v, axis=0, keepdims=True) for v in (middle, middle * middle)]
    sums_ref[...] = sums_ref[...] + jnp.concatenate(sums)[None]


def put_blocks(out_ref, values, shape, order_ref):
    if order_ref is None:
        out_ref[...] = lower(values).reshape(shape)
    else:
        out_ref[...] = lower(dot_tn(lower(values), order_ref[...]))


def output_kernel(ff_ref, branch_ref, cot_ref, vector_ref, *rest):
    order_ref, out_ref, sums_ref = rest if len(rest) == 3 else (None,) + rest
    zero_first(sums_ref)
    row = lambda k: vector_ref[k : k + 1, :]
    ff = flat(ff_ref) + row(1)
    cot = flat(cot_ref).astype(F32)
    put_blocks(out_ref, row(0) * flat(branch_ref) + row(2) * ff, ff_ref.shape, order_ref)
    add_row(sums_ref, 0, cot * ff)
    add_row(sums_ref, 1, lower(cot * row(2)).astype(F32))


def branch_kernel(
    edges,
    dn2_ref,
    middle_ref,
    cot_ref,
    branch_ref,
    gq_ref,
    g_ref,
    t7_ref,
    totals_ref,
    norm_sums_ref,
    vector_ref,
    second_ref,
    third_ref,
    grad_ref,
    gated_ref,
    d7_ref,
    w2_ref,
    w3_ref,
    sums_ref,
    *rest,
):
    edge_refs, (acc2, acc3) = rest[:-2], rest[-2:]
    zero_first(sums_ref, acc2, acc3)
    shape = dn2_ref.shape
    channels = shape[2]
    row = lambda k: vector_ref[k : k + 1, :]
    part = 1.0 / (shape[0] * ROWS * pl.num_programs(0) * totals_ref.shape[0])
    totals = jnp.sum(totals_ref[...], axis=0) * part
    mean = totals[0:1, :]
    rstd = lax.rsqrt(totals[1:2, :] - mean * mean + EPSILON)
    norm_sums = jnp.sum(norm_sums_ref[...], axis=0)
    gain = row(8)
    unit = (flat(middle_ref) - mean) * rstd
    means = norm_sums * part
    norm_grad = (rstd * gain) * (flat(dn2_ref) - means[0:1, :] - unit * means[1:2, :])
    grad_middle = flat(cot_ref).astype(F32) + norm_grad
    grad_ref[...] = norm_grad.reshape(shape)
    add_row(sums_ref, 0, grad_middle * flat(branch_ref))
    low_three = lower(grad_middle * row(7))
    add_row(sums_ref, 1, low_three.astype(F32))
    back_gated = dot_nn(low_three, third_ref[...])
    gated_ref[...] = back_gated.reshape(shape)
    acc3[...] = acc3[...] + dot_tn(low_three, flat(gq_ref))
    low_two = lower(back_gated * flat(g_ref))
    add_row(sums_ref, 2, low_two.astype(F32))
    back_seven = dot_nn(low_two, second_ref[...])
    acc2[...] = acc2[...] + dot_tn(low_two, flat(t7_ref))
    add_row(sums_ref, 3, back_seven)
    d7_ref[...] = lower(back_seven).reshape(shape)
    if edges:
        put_edges(back_seven, shape, *edge_refs)
    sums_ref[4:6, :] = norm_sums

    @pl.when(pl.program_id(0) == pl.num_programs(0) - 1)
    def _():
        blank = jnp.zeros((channels, SIDE_WIDTH), BF16)
        for ref, acc in ((w2_ref, acc2), (w3_ref, acc3)):
            ref[:, :channels] = lower(acc[...])
            ref[:, channels:] = blank


def last_kernel(
    grid_shape,
    back_ref,
    gated_ref,
    q_ref,
    slope_ref,
    unit_ref,
    grad_ref,
    cot_ref,
    vector_ref,
    rstd_ref,
    first_ref,
    out_sums,
    branch_sums,
    bias_three,
    five_part,
    seven_part,
    *rest,
):
    order_ref, out_ref, rows_ref, w1, sums, vectors, rows = (
        rest if len(rest) == 7 else (None,) + rest
    )
    zero_first(w1, sums)
    row = lambda k: vector_ref[k : k + 1, :]
    unit = flat(unit_ref)
    norm_grad = flat(grad_ref)
    low_one = lower((flat(gated_ref) * flat(q_ref) + flat(back_ref)) * flat(slope_ref))
    add_row(sums, 2, low_one.astype(F32))
    grad_branch = (flat(cot_ref).astype(F32) + norm_grad) * row(7)
    grad_normed = grad_branch + dot_nn(low_one, first_ref[...])
    w1[...] = w1[...] + dot_tn(low_one, lower(unit * row(0) + row(1)))
    add_row(sums, 1, grad_normed)
    add_row(sums, 0, grad_normed * unit)
    scale = rstd_ref[...] * row(0)
    put_blocks(out_ref, norm_grad + scale * grad_normed, unit_ref.shape, order_ref)

    @pl.when(pl.program_id(0) == pl.num_programs(0) - 1)
    def _():
        dp, chan, local_chans, each, few = grid_shape
        vectors[...] = jnp.zeros_like(vectors)
        vectors[0:3, :] = sums[0:3, :]
        vectors[3:4, :] = bias_three[...]
        for k in range(4):
            vectors[4 + k : 5 + k, :] = branch_sums[3 - k : 4 - k, :]
        vectors[10:11, :] = out_sums[1:2, :]
        vectors[11:12, :] = out_sums[0:1, :]
        vectors[12:37, :] = five_part[...]
        vectors[37:86, :] = seven_part[...]
        rows[...] = jnp.zeros_like(rows)
        for d in range(dp):
            count = max(0, min(each, local_chans - d * each))
            for k in range(chan):
                i = d * chan + k
                if count:
                    first = k * local_chans + d * each
                    rows[i, 0:count, :] = w1[first : first + count, :]
                rows[i, each : each + few, :] = vectors[i * few : (i + 1) * few, :]
        rows_ref[...] = lower(rows[...])


def lane_spec(shape):
    if len(shape) == 2:
        return pl.BlockSpec((shape[0], LANES), lambda l: (0, l))
    return pl.BlockSpec((shape[0], shape[1], LANES), lambda l: (0, 0, l))


def whole_spec(shape):
    zeros = (0,) * len(shape)
    return pl.BlockSpec(shape, lambda l: zeros)


def tied(kernel, count, ties):
    specs = [pl.BlockSpec(memory_space=pl.ANY)] * len(ties)
    if not ties:
        return kernel, specs
    return lambda *refs: kernel(*refs[:count], *refs[count + len(ties) :]), specs


def lane_call(kernel, inputs, outputs, scratch, microseconds, name, ties=()):
    channels = outputs[0].shape[-1]
    kernel, tie_specs = tied(kernel, len(inputs), ties)
    return pl.pallas_call(
        kernel,
        grid=(pl.cdiv(channels, LANES),),
        in_specs=[lane_spec(v.shape) if lanes else whole_spec(v.shape) for v, lanes in inputs]
        + tie_specs,
        out_specs=[lane_spec(v.shape) for v in outputs],
        out_shape=outputs,
        scratch_shapes=scratch,
        compiler_params=pltpu.CompilerParams(vmem_limit_bytes=VMEM_LIMIT),
        cost_estimate=cost(microseconds),
        name=name,
    )(*[v for v, _ in inputs], *ties)


def attention_forward(g_parts, taps, biases, five, seven, valid):
    width, height, channels = g_parts[1].shape
    return lane_call(
        functools.partial(attention_forward_kernel, width),
        [(v, True) for v in (*g_parts, taps, biases)] + [(v, False) for v in (five, seven, valid)],
        [
            jax.ShapeDtypeStruct((width + 18, height, channels), BF16),
            jax.ShapeDtypeStruct((width, height, channels), BF16),
        ],
        [
            pltpu.VMEM((74, 2 * SUB, LANES), BF16),
            pltpu.VMEM((width + 22, height, LANES), BF16),
        ],
        23,
        "attention_forward",
    )


def attention_backward(d7_parts, taps, five, seven, valid, ties):
    width, height, channels = d7_parts[1].shape
    return lane_call(
        functools.partial(attention_backward_kernel, width),
        [(v, True) for v in (*d7_parts, taps)] + [(v, False) for v in (five, seven, valid)],
        [
            jax.ShapeDtypeStruct((width, height, channels), F32),
            jax.ShapeDtypeStruct((width, height, channels), BF16),
            jax.ShapeDtypeStruct((1, channels), F32),
        ],
        [
            pltpu.VMEM((74, 2 * SUB, LANES), BF16),
            pltpu.VMEM((width + 24, height, LANES), BF16),
            pltpu.VMEM((width + 6, height, LANES), BF16),
        ],
        21,
        "attention_backward",
        ties,
    )


def tap_sums_seven(d7, t5_ext, seven, ties):
    width, height, channels = d7.shape
    return lane_call(
        functools.partial(tap_seven_kernel, width),
        [(d7, True), (t5_ext, True), (seven, False)],
        [jax.ShapeDtypeStruct((49, channels), F32)],
        [],
        16,
        "tap_sums_seven",
        ties,
    )[0]


def tap_sums_five(d5, g_parts, five, ties):
    width, height, channels = d5.shape
    return lane_call(
        functools.partial(tap_five_kernel, width),
        [(v, True) for v in (d5, *g_parts)] + [(five, False)],
        [jax.ShapeDtypeStruct((25, channels), F32)],
        [pltpu.VMEM((width + 4, height, LANES), BF16)],
        7,
        "tap_sums_five",
        ties,
    )[0]


def mlp_both(mid_parts, cot, totals, vectors, pair, biases, taps, three, valid):
    width, height, channels = mid_parts[1].shape
    hidden = pair.shape[0] * pair.shape[1] // 2
    tile = HIDDEN_TILE
    own = width * height
    size = 2 if width % 2 == 0 else 1

    def rows_spec(columns):
        return pl.BlockSpec((tile, columns), lambda t: (t, 0))

    def lanes_spec(rows):
        return pl.BlockSpec((rows, tile), lambda t: (0, t))

    whole = [*mid_parts, cot, totals, vectors, pair]
    wide = channels + SIDE_WIDTH
    return pl.pallas_call(
        functools.partial(mlp_kernel_body, width, height),
        grid=(hidden // tile,),
        in_specs=[whole_spec(v.shape) for v in whole]
        + [
            lanes_spec(2),
            lanes_spec(9),
            whole_spec(three.shape),
            whole_spec(valid.shape),
        ],
        out_specs=[
            whole_spec((own, channels)),
            whole_spec((own, channels)),
            rows_spec(wide),
            rows_spec(wide),
            whole_spec(totals.shape),
        ],
        out_shape=[
            jax.ShapeDtypeStruct((own, channels), F32),
            jax.ShapeDtypeStruct((own, channels), F32),
            jax.ShapeDtypeStruct((hidden, wide), BF16),
            jax.ShapeDtypeStruct((hidden, wide), BF16),
            jax.ShapeDtypeStruct(totals.shape, F32),
        ],
        scratch_shapes=[
            pltpu.VMEM((9, 2 * SUB, tile), BF16),
            pltpu.VMEM(((width + 4 + size) * height, channels), BF16),
            pltpu.VMEM(((width + 2) * height, channels), BF16),
            pltpu.VMEM((width + 4 + size, height, tile), BF16),
            pltpu.VMEM((width + 2, height, tile), BF16),
            pltpu.VMEM(((width + 2 + size) * height, tile), BF16),
            pltpu.VMEM(((width + size) * height, tile), BF16),
            pltpu.VMEM(((width + 2 + size) * height, channels), F32),
            pltpu.VMEM(((width + size) * height, channels), F32),
            pltpu.VMEM((9, SUB, tile), F32),
            pltpu.VMEM((2, SUB, tile), F32),
            pltpu.VMEM((tile, channels), BF16),
            pltpu.VMEM((tile, channels), BF16),
        ],
        compiler_params=pltpu.CompilerParams(vmem_limit_bytes=VMEM_LIMIT),
        cost_estimate=cost(60),
        name="mlp_both",
    )(*whole, biases, taps, three, valid)


SEGMENT = 24
ROWS = 16
BLOCK = SEGMENT * ROWS
SLOTS = LANES // SEGMENT


def vmem_call(kernel, out_shape, scratch, microseconds, name, *operands, ties=()):
    kernel, tie_specs = tied(kernel, len(operands), ties)
    return pl.pallas_call(
        kernel,
        out_shape=out_shape,
        in_specs=[pl.BlockSpec(memory_space=pltpu.VMEM)] * len(operands) + tie_specs,
        out_specs=jax.tree.map(lambda _: pl.BlockSpec(memory_space=pltpu.VMEM), out_shape),
        scratch_shapes=scratch,
        compiler_params=pltpu.CompilerParams(vmem_limit_bytes=VMEM_LIMIT),
        cost_estimate=cost(microseconds),
        name=name,
    )(*operands, *ties)


def lane_index():
    return lax.broadcasted_iota(jnp.int32, (SUB, LANES), 1)


def choose(mask, first, second):
    rows = first.shape[0]
    pair = [v.reshape(rows // SUB, SUB, LANES) for v in (first, second)]
    return jnp.where(mask[None], *pair).reshape(rows, LANES)


def tile_of(index):
    return slice(index * LANES, (index + 1) * LANES)


def pack_kernel(device_of, centre, x_ref, swap_ref, out_ref, mean_ref, square_ref, y, last):
    chans, rows, columns = x_ref.shape
    count = rows * columns
    for i in range(chans // SUB):
        part = slice(i * SUB, (i + 1) * SUB)
        values = x_ref[part]
        if centre:
            mean = jnp.sum(values, axis=(1, 2), keepdims=True) * (1.0 / count)
            values = values - mean
            square = jnp.sum(values * values, axis=(1, 2), keepdims=True)
            mean_ref[part] = jnp.broadcast_to(mean, (SUB, 1, LANES))
            square_ref[part] = jnp.broadcast_to(square, (SUB, 1, LANES))
        swapped = dot_nn(swap_ref[...], lower(values).reshape(SUB * rows, columns))
        y[:, part, :] = swapped.reshape(rows, SUB, columns)
    for t in range(columns // LANES):
        for tile in range(3):
            last[tile, :, tile_of(t)] = pltpu.roll(
                y[rows - 1, :, tile_of(t)], LANES - SUB * (tile + 1), 1
            )
        for r in range(rows - 1):
            if r % SLOTS:
                y[r, :, tile_of(t)] = pltpu.roll(y[r, :, tile_of(t)], SEGMENT * (r % SLOTS), 1)
    for s, device in enumerate(device_of):
        t, start = divmod(s * SEGMENT, LANES)
        place = (lane_index() - start) & (LANES - 1)
        over = LANES - start
        for tile in range(3):
            pieces = []
            for m in range(SLOTS):
                piece = y[tile * SLOTS + m, :, tile_of(t)]
                if over < SEGMENT:
                    beyond = y[tile * SLOTS + m, :, tile_of(t + 1)]
                    piece = choose(place - SEGMENT * m >= over, beyond, piece)
                pieces.append(piece)
            value = pieces[-1]
            for m in range(SLOTS - 2, -1, -1):
                value = choose(place < SEGMENT * (m + 1), pieces[m], value)
            source = t if start + SUB * tile < LANES else t + 1
            value = choose(place >= SEGMENT * SLOTS, last[tile, :, tile_of(source)], value)
            out_ref[device, :, tile_of(tile)] = lower(value)


def drop_stats(kernel, x_ref, swap_ref, out_ref, y, last):
    kernel(x_ref, swap_ref, out_ref, None, None, y, last)


def unpack_kernel(device_of, affine, got_ref, swap_ref, part_ref, base_ref, *rest):
    if affine:
        x_ref, coef_ref, out_ref, flat, y = rest
    else:
        out_ref, flat, y = rest
    chans, rows, columns = out_ref.shape
    flat[...] = got_ref[...].astype(F32)
    for t in range(columns // LANES):
        strips = []
        for s, device in enumerate(device_of):
            end = (s + 1) * SEGMENT - t * LANES
            if end > 0 and s * SEGMENT - t * LANES < LANES:
                strips.append((end, device))

        def pick(place, tile, strips=strips):
            value = flat[strips[-1][1], :, tile_of(tile)]
            for end, device in strips[-2::-1]:
                value = choose(place < end, flat[device, :, tile_of(tile)], value)
            return value

        for m in range(SLOTS):
            place = (lane_index() - SEGMENT * m) & (LANES - 1)
            for tile in range(3):
                value = pick(place, tile)
                if m:
                    value = pltpu.roll(value, LANES - SEGMENT * m, 1)
                y[tile * SLOTS + m, :, tile_of(t)] = value
        pieces = []
        for tile in range(3):
            place = (lane_index() + SUB * (tile + 1)) & (LANES - 1)
            pieces.append(pltpu.roll(pick(place, tile), SUB * (tile + 1), 1))
        part = part_ref[t]
        value = choose(part == 0, pieces[0], choose(part == 1, pieces[1], pieces[2]))
        y[rows - 1, :, tile_of(t)] = value
    for i in range(chans // SUB):
        part = slice(i * SUB, (i + 1) * SUB)
        mixed = lower(y[:, part, :]).reshape(SUB * rows, columns)
        value = dot_nn(swap_ref[...], mixed).reshape(SUB, rows, columns)
        if affine:
            for t in range(columns // LANES):
                lanes = tile_of(t)
                out_ref[part, :, lanes] = (
                    base_ref[part, :, lanes]
                    + value[:, :, lanes]
                    - coef_ref[0, part]
                    - coef_ref[1, part] * (x_ref[part, :, lanes] - coef_ref[2, part])
                )
        else:
            out_ref[part] = base_ref[part] + value


def first_kernel(
    got_ref,
    order_ref,
    offset_ref,
    vector_ref,
    weight_ref,
    unit_ref,
    g_ref,
    slope_ref,
    low_ref,
    *edge_refs,
):
    values = dot_nt(order_ref[...], got_ref[...])
    unit = values * vector_ref[0:1, :] + offset_ref[...]
    normed = unit * vector_ref[1:2, :] + vector_ref[2:3, :]
    first = dot_nt(lower(normed), weight_ref[...]) + vector_ref[3:4, :]
    active, slope = gelu_parts(first)
    shape = unit_ref.shape
    unit_ref[...] = unit.reshape(shape)
    g_ref[...] = active.reshape(shape)
    slope_ref[...] = slope.reshape(shape)
    low_ref[...] = lower(active).reshape(shape)
    put_edges(active, shape, *edge_refs)


def finish_kernel(
    shrink,
    up_rate,
    early_ref,
    last_ref,
    up_momentum,
    down_rows,
    first_momentum,
    second_momentum,
    third_momentum,
    up_weight,
    down_weight,
    square_weights,
    new_up,
    new_down,
    new_squares,
):
    new_up[...] = shrink * up_weight[...] - up_rate * dot_nn(
        lower(up_momentum[...]), early_ref[0]
    )
    new_down[...] = shrink * down_weight[...] - MATRIX_RATE * dot_nt(
        early_ref[1], lower(down_rows[...])
    )
    first = dot_split(split_low(first_momentum[...]), split_low(last_ref[...]))
    second = dot_nn(lower(second_momentum[...]), early_ref[2])
    third = dot_nn(lower(third_momentum[...]), early_ref[3])
    for k, ortho in enumerate((first, second, third)):
        new_squares[k] = shrink * square_weights[k] - MATRIX_RATE * ortho


class Strips:
    def __init__(self, local_chans, local_rows, columns):
        self.dp = lax.axis_size("dp")
        self.chan = lax.axis_size("chan")
        self.count = self.dp * self.chan
        self.local_chans = local_chans
        self.local_rows = local_rows
        self.columns = columns
        self.width = columns // self.count
        self.height = local_rows * self.dp
        self.channels = local_chans * self.chan
        self.device_of = []
        for d in range(self.dp):
            line = list(range(d * self.chan, (d + 1) * self.chan))
            self.device_of += line if d % 2 == 0 else line[::-1]
        d = lax.axis_index("dp")
        c = lax.axis_index("chan")
        self.index = d * self.chan + jnp.where(d % 2 == 0, c, self.chan - 1 - c)
        self.steps = self.height // ROWS
        self.fast = (
            self.width == SEGMENT
            and local_rows == ROWS
            and local_chans % SUB == 0
            and columns % LANES == 0
        )
        if self.fast:
            self.prepare()

    def prepare(self):
        mixed = np.arange(SUB * ROWS)
        swap = np.zeros((SUB * ROWS, SUB * ROWS), np.float32)
        swap[mixed, (mixed % SUB) * ROWS + mixed // SUB] = 1.0
        self.swap = jnp.asarray(swap, BF16)
        self.swap_back = jnp.asarray(swap.T, BF16)
        part = (np.arange(self.columns) % SEGMENT) // SUB
        part = part.reshape(-1, 1, LANES).astype(np.int32)
        self.part = jnp.asarray(np.broadcast_to(part, (part.shape[0], SUB, LANES)))
        start = (self.index * SEGMENT) % LANES
        w, r = np.divmod(np.arange(BLOCK), ROWS)
        last = r == ROWS - 1
        tile = np.where(last, w // SUB, r // SLOTS)
        shift = np.where(last, w % SUB - SUB, SEGMENT * (r % SLOTS) + w)
        lane = LANES * jnp.asarray(tile) + (start + jnp.asarray(shift)) % LANES
        self.order = (lane[:, None] == jnp.arange(BLOCK)[None, :]).astype(BF16)

    def pack(self, values, centre, ties=()):
        chans, rows, columns = values.shape
        blocks = jax.ShapeDtypeStruct((self.count, chans, BLOCK), BF16)
        stat = jax.ShapeDtypeStruct((chans, 1, LANES), F32)
        scratch = [pltpu.VMEM((rows, chans, columns), F32), pltpu.VMEM((3, chans, columns), F32)]
        kernel = functools.partial(pack_kernel, self.device_of, centre)
        if not centre:
            kernel = functools.partial(drop_stats, kernel)
            out = [blocks]
        else:
            out = [blocks, stat, stat]
        return vmem_call(kernel, out, scratch, 4, "pack", values, self.swap, ties=ties)

    def unpack(self, got, base, *affine, ties=()):
        scratch = [pltpu.VMEM(got.shape, F32), pltpu.VMEM((ROWS,) + base.shape[:1] + base.shape[2:], F32)]
        kernel = functools.partial(unpack_kernel, self.device_of, bool(affine))
        return vmem_call(
            kernel,
            jax.ShapeDtypeStruct(base.shape, F32),
            scratch,
            5,
            "unpack",
            got,
            self.swap_back,
            self.part,
            base,
            *affine,
            ties=ties,
        )

    def move(self, blocks):
        return lax.all_to_all(blocks, BOTH, split_axis=0, concat_axis=0, tiled=True)

    def stage(self, kernel, inputs, outputs, microseconds, name, scratch=(), ties=()):
        kernel, tie_specs = tied(kernel, len(inputs), ties)

        def spec(value):
            shape = value.shape
            if len(shape) == 3 and shape[1:] == (self.height, self.channels):
                return pl.BlockSpec((shape[0], ROWS, shape[2]), lambda d: (0, d, 0))
            if len(shape) == 3 and shape[0] == self.steps:
                return pl.BlockSpec((None,) + shape[1:], lambda d: (d, 0, 0))
            return whole_spec(shape)

        return pl.pallas_call(
            kernel,
            grid=(self.steps,),
            in_specs=[spec(v) for v in inputs] + tie_specs,
            out_specs=jax.tree.map(spec, outputs),
            out_shape=outputs,
            scratch_shapes=scratch,
            compiler_params=pltpu.CompilerParams(vmem_limit_bytes=VMEM_LIMIT),
            cost_estimate=cost(microseconds),
            name=name,
        )(*inputs, *ties)

    def strips(self, dtype, columns=None):
        return jax.ShapeDtypeStruct((columns or self.width, self.height, self.channels), dtype)

    def edge_shapes(self, reach):
        return [self.strips(BF16, reach)] * 2 if reach <= self.width else []

    def blocks(self):
        return jax.ShapeDtypeStruct((self.steps, self.channels, BLOCK), BF16)

    def per_step(self, got):
        return got.reshape(self.steps, self.channels, BLOCK)

    def sums(self, rows):
        return jax.ShapeDtypeStruct((rows, self.channels), F32)

    def first_stage(self, got, offset, vectors, weight, ties):
        inputs = [self.per_step(got), self.order, offset[:, None, :], vectors, weight]
        outputs = [self.strips(F32)] * 3 + [self.strips(BF16)] + self.edge_shapes(11)
        unit, active, slope, low, *edges = self.stage(
            first_kernel, inputs, outputs, 7, "first_stage", ties=ties
        )
        return unit, active, slope, low, edges

    def leave(self):
        if self.fast:
            return [self.order], self.blocks()
        return [], self.strips(BF16)

    def reorder(self, blocks):
        lines = blocks.reshape((self.dp, self.chan) + blocks.shape[1:])
        lines = [lines[d] if d % 2 == 0 else lines[d][::-1] for d in range(self.dp)]
        return jnp.concatenate(lines, axis=0)

    def exchange(self, blocks):
        size = math.prod(blocks.shape[1:])
        shape = blocks.shape
        flat = (size // LANES, LANES) if size % LANES == 0 else (size,)
        moved = lax.all_to_all(
            blocks.reshape((self.count,) + flat), BOTH, split_axis=0, concat_axis=0, tiled=True
        )
        return moved.reshape(shape)

    def to_strips(self, values):
        blocks = values.reshape(self.local_chans, self.local_rows, self.count, self.width)
        blocks = self.reorder(jnp.transpose(blocks, (2, 0, 1, 3)))
        got = self.exchange(blocks)
        got = got.reshape(self.dp, self.chan, self.local_chans, self.local_rows, self.width)
        got = jnp.transpose(got, (4, 0, 3, 1, 2))
        return got.reshape(self.width, self.height, self.channels)

    def from_strips(self, values):
        blocks = values.reshape(self.width, self.dp, self.local_rows, self.chan, self.local_chans)
        blocks = jnp.transpose(blocks, (1, 3, 4, 2, 0))
        blocks = blocks.reshape(self.count, self.local_chans, self.local_rows, self.width)
        got = self.reorder(self.exchange(blocks))
        got = jnp.transpose(got, (1, 2, 0, 3))
        return got.reshape(self.local_chans, self.local_rows, self.columns)

    def halo(self, values, reach, edges=()):
        steps = -(-reach // self.width)
        left, right = [], []
        for step in range(1, steps + 1):
            take = min(self.width, reach - (step - 1) * self.width)
            forth = [
                (self.device_of[s], self.device_of[s + step]) for s in range(self.count - step)
            ]
            low, high = edges or (values[:take], values[self.width - take :])
            left.insert(0, lax.ppermute(high, BOTH, forth))
            right.append(lax.ppermute(low, BOTH, [(b, a) for a, b in forth]))
        if steps == 1:
            return left[0], values, right[0]
        return jnp.concatenate(left), values, jnp.concatenate(right)


def split_low(values):
    high = lower(values)
    return high, lower(values - high.astype(F32))


def dot_split(left, right):
    (left_high, left_low), (right_high, right_low) = left, right
    rows = left_high.shape[0]
    both = dot_nn(jnp.concatenate([left_high, left_low]), right_high)
    return both[:rows] + both[rows:] + dot_nn(left_high, right_low)


def factor_kernel(limit, rows_ref, factor_ref, gram, factor):
    size = gram.shape[0]
    eye = (
        lax.broadcasted_iota(jnp.int32, (size, size), 0)
        == lax.broadcasted_iota(jnp.int32, (size, size), 1)
    ).astype(F32)
    rows = rows_ref[...]
    if limit is not None:
        row = lax.broadcasted_iota(jnp.int32, rows.shape[1:], 0)
        rows = jnp.where((row < limit)[None], rows.astype(F32), 0.0).astype(BF16)
        rows = rows.reshape(-1, size)
    first = dot_tn(rows, rows)
    norm_value = jnp.sqrt(jnp.sum(first * eye, keepdims=True)) + 1e-07
    scale = 1.0 / norm_value
    gram[...] = first * (scale * scale)

    def polynomial_of(now, pair):
        square = dot_split(pair, pair)
        return square, ORDER_ONE * eye + ORDER_THREE * now + ORDER_FIVE * square

    def advance(step, carry):
        now = gram[...]
        pair = split_low(now)
        square, polynomial = polynomial_of(now, pair)
        cube = dot_split(pair, split_low(square))
        half = ORDER_ONE * now + ORDER_THREE * square + ORDER_FIVE * cube
        old = jnp.where(step == 0, eye * scale, factor[...])
        product = dot_split(split_low(jnp.concatenate([half, old])), split_low(polynomial))
        gram[...] = product[:size]
        factor[...] = product[size:]
        return carry

    factor[...] = eye
    lax.fori_loop(0, SCHULZ_STEPS - 1, advance, 0)
    now = gram[...]
    _, polynomial = polynomial_of(now, split_low(now))
    factor_ref[...] = dot_split(split_low(factor[...]), split_low(polynomial))


def orthogonal_factor(rows, ties=(), limit=None):
    size = rows.shape[-1]
    kernel, tie_specs = tied(functools.partial(factor_kernel, limit), 1, ties)
    return pl.pallas_call(
        kernel,
        out_shape=jax.ShapeDtypeStruct((size, size), F32),
        in_specs=[pl.BlockSpec(memory_space=pltpu.VMEM)] + tie_specs,
        out_specs=pl.BlockSpec(memory_space=pltpu.VMEM),
        scratch_shapes=[pltpu.VMEM((size, size), F32), pltpu.VMEM((size, size), F32)],
        compiler_params=pltpu.CompilerParams(vmem_limit_bytes=VMEM_LIMIT),
        cost_estimate=cost(13),
        name="orthogonal_factor",
    )(rows, *ties)


def behind(values, *earlier):
    any_spec = pl.BlockSpec(memory_space=pl.ANY)
    return pl.pallas_call(
        lambda *refs: None,
        out_shape=jax.ShapeDtypeStruct(values.shape, values.dtype),
        in_specs=[any_spec] * (1 + len(earlier)),
        out_specs=any_spec,
        input_output_aliases={0: 0},
        cost_estimate=cost(0.1),
        name="behind",
    )(values, *earlier)


def share(values, axes):
    count = lax.axis_size(axes)
    copies = jnp.broadcast_to(values[None], (count,) + values.shape)
    return lax.all_to_all(copies, axes, split_axis=0, concat_axis=0, tiled=True)


def exchange(values, axis):
    return lax.all_to_all(values, axis, split_axis=0, concat_axis=0, tiled=True)


def turns(values, axis):
    count = lax.axis_size(axis)
    return [
        lax.ppermute(values, axis, [(i, (i + r) % count) for i in range(count)])
        for r in range(count - 1, 0, -1)
    ] + [values]


def share_by_turns(values, axis):
    count = lax.axis_size(axis)
    if count > 8:
        return lax.all_gather(values, axis)
    got = turns(values, axis)
    start = count - 1 - lax.axis_index(axis)
    return lax.dynamic_slice_in_dim(jnp.stack(got + got), start, count, axis=0)


def share_dp(values):
    return share_by_turns(values, "dp")


def scatter_dp(blocks):
    count = lax.axis_size("dp")
    here = lax.axis_index("dp")

    def block(step):
        return lax.dynamic_index_in_dim(blocks, (here + step) % count, axis=0, keepdims=False)

    result = block(0).astype(F32)
    for step in range(1, count):
        pairs = [(i, (i + step) % count) for i in range(count)]
        result = result + lax.ppermute(block(step), "dp", pairs).astype(F32)
    return result


def share_rows(rows):
    chan = lax.axis_size("chan")
    count = rows.shape[0]
    if chan > 8 or count % (4 * SUB):
        return share(rows, "chan").reshape(-1, rows.shape[1])
    half = count // 2
    parity = lax.axis_index("chan") % 2
    across = [(i, i ^ 1) for i in range(chan)]
    kept = lax.dynamic_slice_in_dim(rows, parity * half, half, axis=0)
    sent = lax.dynamic_slice_in_dim(rows, (1 - parity) * half, half, axis=0)
    held = jnp.concatenate([kept, lax.ppermute(sent, "chan", across)])
    held = jnp.concatenate(
        [held]
        + [
            lax.ppermute(held, "chan", [(i, (i + 2 * step) % chan) for i in range(chan)])
            for step in range(1, chan // 2)
        ]
    )
    return jnp.concatenate([held, lax.ppermute(held, "chan", across)])


def for_dp(parts):
    dp = lax.axis_size("dp")
    blocks = []
    for part in parts:
        chan, rows, lanes = part.shape
        each = -(-rows // (SUB * dp)) * SUB
        part = jnp.pad(part, ((0, 0), (0, each * dp - rows), (0, 0)))
        blocks.append(part.reshape(chan, dp, each, lanes))
    return jnp.concatenate(blocks, axis=2)


def scattered(blocks, *earlier):
    chan, dp, rows, lanes = blocks.shape
    parity = lax.axis_index("chan") % 2
    blocks = blocks.reshape(chan // 2, 2, dp, rows, lanes)
    kept = lax.dynamic_index_in_dim(blocks, parity, axis=1, keepdims=False)
    sent = lax.dynamic_index_in_dim(blocks, 1 - parity, axis=1, keepdims=False)
    got = behind(lax.ppermute(sent, "chan", [(i, i ^ 1) for i in range(chan)]), *earlier)
    both = lower(kept.astype(F32) + got.astype(F32))
    return lower(scatter_dp(jnp.transpose(both, (1, 0, 2, 3))))


def summed_over_chan(blocks, *earlier):
    half = blocks.shape[0]
    place = lax.axis_index("chan") // 2

    def block(step):
        return lax.dynamic_index_in_dim(blocks, (place + step) % half, axis=0, keepdims=False)

    result = block(0).astype(F32)
    for step in range(1, half):
        pairs = [(i, (i + 2 * step) % (2 * half)) for i in range(2 * half)]
        got = lax.ppermute(block(step), "chan", pairs)
        if step == 1:
            got = behind(got, *earlier)
        result = result + got.astype(F32)
    return lower(result)


def own_rows(rows, counts):
    dp = lax.axis_size("dp")
    got = share_dp(rows).astype(F32)
    out, place = [], 0
    for count in counts:
        each = -(-count // (SUB * dp)) * SUB
        out.append(got[:, place : place + each].reshape(dp * each, -1)[:count])
        place += each
    return out


def body(
    block_input,
    cotangent,
    canvas_rows,
    square_weights,
    square_momenta,
    up_weight,
    up_momentum,
    down_weight,
    down_momentum,
    narrow_vectors,
    narrow_momenta,
    wide_vectors,
    wide_momenta,
    lka_kernels,
    lka_momenta,
    mlp_kernel,
    mlp_momentum,
):
    local_chans, local_rows, columns = block_input.shape
    hidden_local = up_weight.shape[0]
    grid = Strips(local_chans, local_rows, columns)
    width, height, channels = grid.width, grid.height, grid.channels
    hidden = hidden_local * grid.chan
    own = width * height
    pixel_count = height * columns
    local_count = local_rows * columns
    here = lax.axis_index("chan")


    if grid.fast:
        blocks, local_mean, local_square = grid.pack(block_input, True)
        local_mean, local_square = local_mean[:, 0, 0], local_square[:, 0, 0]
        sent_x = grid.move(blocks)
    else:
        local_mean = jnp.sum(block_input, axis=(1, 2)) / local_count
        centred = block_input - local_mean[:, None, None]
        local_square = jnp.sum(centred * centred, axis=(1, 2))
        sent_x = grid.to_strips(lower(centred))
    stats = share_dp(jnp.stack([local_mean, local_square]))
    own_mean = jnp.mean(stats[:, 0], axis=0)
    apart = stats[:, 0] - own_mean
    variance = (jnp.sum(stats[:, 1], axis=0) + local_count * jnp.sum(apart * apart, axis=0)) / (
        pixel_count
    )
    own_rstd = lax.rsqrt(variance + EPSILON)

    fold = hidden_local // local_chans
    vectors = jnp.concatenate(
        [
            own_rstd[:, None],
            (apart * own_rstd).T,
            narrow_vectors.T,
            lka_kernels,
            jnp.transpose(wide_vectors.reshape(2, fold, local_chans), (2, 0, 1)).reshape(
                local_chans, -1
            ),
            jnp.transpose(mlp_kernel.reshape(fold, local_chans, 9), (1, 2, 0)).reshape(
                local_chans, -1
            ),
        ],
        axis=1,
    )
    count = vectors.shape[1]
    high = lax.reduce_precision(vectors, exponent_bits=8, mantissa_bits=7)
    vectors = lower(jnp.concatenate([high, vectors - high], axis=1))
    vectors = jnp.pad(vectors, ((0, 0), (0, channels - 2 * count)))
    packed = lax.all_gather(
        jnp.concatenate([lower(square_weights).reshape(3 * local_chans, channels), vectors]), "chan"
    )
    low_one, low_two, low_three = (
        packed[:, k * local_chans : (k + 1) * local_chans].reshape(channels, channels)
        for k in range(3)
    )
    vectors = packed[:, 3 * local_chans : 4 * local_chans].astype(F32)
    vectors = vectors[:, :, :count] + vectors[:, :, count : 2 * count]
    vectors = vectors.reshape(channels, count).T
    rstd_one, spread = vectors[0], vectors[1 : 1 + grid.dp]
    vectors = vectors[1 + grid.dp :]
    narrow, lka_taps = vectors[:12], vectors[12:86]
    hidden_rows = vectors[86:].reshape(11, fold, grid.chan, local_chans)
    hidden_rows = jnp.transpose(hidden_rows, (0, 2, 1, 3)).reshape(11, hidden)
    wide, mlp_taps = hidden_rows[:2], hidden_rows[2:]

    if grid.fast:
        unit_one, gated_in, first_slope, gated_low, edges = grid.first_stage(
            sent_x,
            spread,
            jnp.concatenate([rstd_one[None], narrow[:3]]),
            low_one,
            (),
        )
    else:
        offset = jnp.repeat(spread, local_rows, axis=0)
        unit_one = sent_x.astype(F32) * rstd_one + offset
        low_normed = lower(unit_one * narrow[0] + narrow[1]).reshape(own, channels)
        first = dot_nt(low_normed, low_one) + narrow[2]
        gated_in, first_slope = (v.reshape(unit_one.shape) for v in gelu_parts(first))
        gated_low = lower(gated_in)
        edges = ()
    g_parts = grid.halo(gated_low, 11, edges)

    masks_five, masks_seven, masks_three, valid = make_masks(
        canvas_rows, grid.index, height, columns, width, [gated_low]
    )

    if grid.fast:
        cot_blocks = grid.pack(cotangent, False, [gated_low])[0]
        cot_got = grid.move(behind(cot_blocks, g_parts[0], g_parts[2]))
    t5_ext, after_seven = attention_forward(
        g_parts, lka_taps, narrow[3:5], masks_five, masks_seven, valid
    )
    pair = jnp.concatenate([lower(up_weight), lower(down_weight.T)])
    if grid.fast:
        pair = behind(pair, cot_got, after_seven)
    pair = lax.all_gather(pair, "chan")
    if hidden_local % (4 * SUB):
        pair = [pair[:, :hidden_local], pair[:, hidden_local:]]
        pair = jnp.concatenate([v.reshape(hidden, channels) for v in pair])[None]
    if grid.fast:
        leaving = [grid.per_step(cot_got), grid.order]
        unpacked = [grid.strips(BF16)]
    else:
        cot = grid.to_strips(lower(cotangent))
        leaving, unpacked = [cot], []
    q, gated, branch_one, middle, totals, low_edge, high_edge, *unpacked = grid.stage(
        functools.partial(middle_kernel, grid.fast),
        [
            after_seven,
            gated_in,
            unit_one,
            jnp.concatenate([(1.0 / rstd_one)[None], narrow[:2], narrow[5:8]]),
            low_two,
            low_three,
            *leaving,
        ],
        [grid.strips(F32), grid.strips(BF16), grid.strips(F32), grid.strips(F32)]
        + [jax.ShapeDtypeStruct((grid.count, 2, channels), F32)]
        + [grid.strips(BF16, 3)] * 2
        + unpacked,
        8,
        "middle_stage",
    )
    cot = unpacked[0] if grid.fast else cot

    totals = exchange(totals, BOTH)
    mid_parts = grid.halo(middle, 3, (low_edge, high_edge))
    ff, back_norm, up_part, down_part, norm_sums = mlp_both(
        mid_parts,
        cot,
        totals,
        narrow,
        pair,
        wide,
        mlp_taps,
        masks_three,
        valid,
    )
    extra, leaving = grid.leave()
    out_part, out_sums = grid.stage(
        output_kernel,
        [
            ff.reshape(unit_one.shape),
            branch_one,
            cot,
            jnp.stack([narrow[7], narrow[10], narrow[11]]),
            *extra,
        ],
        [leaving, grid.sums(2)],
        5,
        "output_stage",
    )

    def rows_for(part, rows):
        return part.reshape(grid.chan, rows, -1)

    norm_sums = exchange(norm_sums, BOTH)

    norm_grad, back_gated, back_seven, weight_two, weight_three, branch_sums, *rest = grid.stage(
        functools.partial(branch_kernel, width >= 12),
        [
            back_norm.reshape(unit_one.shape),
            middle,
            cot,
            branch_one,
            gated,
            gated_in,
            after_seven,
            totals,
            norm_sums,
            narrow,
            low_two,
            low_three,
        ],
        [
            grid.strips(F32),
            grid.strips(F32),
            grid.strips(BF16),
            jax.ShapeDtypeStruct((channels, channels + SIDE_WIDTH), BF16),
            jax.ShapeDtypeStruct((channels, channels + SIDE_WIDTH), BF16),
            grid.sums(6),
        ]
        + grid.edge_shapes(12),
        8,
        "branch_stage",
        [pltpu.VMEM((channels, channels), F32)] * 2,
        [out_part],
    )
    d7_parts = grid.halo(back_seven, 12, rest)
    if grid.fast:
        out_blocks = out_part.reshape(grid.count, local_chans, BLOCK)
        out_got = grid.move(out_blocks)
    else:
        out_got = grid.from_strips(out_part)
        block_output = block_input + out_got.astype(F32)

    seven_part = tap_sums_seven(back_seven, t5_ext, masks_seven, ())
    back_g, d5, bias_three = attention_backward(
        d7_parts, lka_taps, masks_five, masks_seven, valid, [seven_part]
    )
    dp_sums = scattered(
        for_dp(
            [
                rows_for(up_part, hidden_local),
                rows_for(down_part, hidden_local),
                jnp.concatenate(
                    [rows_for(weight_two, local_chans), rows_for(weight_three, local_chans)], axis=1
                ),
            ]
        ),
        seven_part,
    )
    five_part = tap_sums_five(d5, g_parts, masks_five, [out_got])
    extra, leaving = grid.leave()
    each = -(-local_chans // grid.dp)
    few = -(-86 // grid.count)
    row_count = -(-(each + few) // (2 * SUB)) * (2 * SUB)
    in_part, last_rows = grid.stage(
        functools.partial(last_kernel, (grid.dp, grid.chan, local_chans, each, few)),
        [
            back_g,
            back_gated,
            q,
            first_slope,
            unit_one,
            norm_grad,
            cot,
            narrow,
            rstd_one[None],
            low_one,
            out_sums,
            branch_sums,
            bias_three,
            five_part,
            seven_part,
            *extra,
        ],
        [leaving, jax.ShapeDtypeStruct((grid.count, row_count, channels), BF16)],
        7,
        "last_stage",
        [
            pltpu.VMEM((channels, channels), F32),
            pltpu.VMEM((SUB, channels), F32),
            pltpu.VMEM((grid.count * few, channels), F32),
            pltpu.VMEM((grid.count, row_count, channels), F32),
        ],
    )
    chan_sums = summed_over_chan(behind(dp_sums, bias_three), last_rows)
    grads = own_rows(chan_sums, [hidden_local, hidden_local, 2 * local_chans])
    up_grad, side_grad = grads[0][:, :channels], grads[0][:, channels : channels + 11]
    down_grad = grads[1][:, :channels]
    second_grad = grads[2][:local_chans, :channels]
    third_grad = grads[2][local_chans:, :channels]
    second_momentum = MATRIX_MOMENTUM * square_momenta[1] + second_grad
    third_momentum = MATRIX_MOMENTUM * square_momenta[2] + third_grad
    new_up_momentum = MATRIX_MOMENTUM * up_momentum + up_grad
    down_rows = MATRIX_MOMENTUM * down_momentum.T + down_grad

    tall = [new_up_momentum, down_rows, second_momentum, third_momentum]
    tall = [jnp.pad(lower(v), ((0, hidden_local - v.shape[0]), (0, 0))) for v in tall]
    mine_of_four = lax.dynamic_index_in_dim(
        jnp.stack(tall), jnp.minimum(lax.axis_index("dp"), len(tall) - 1), keepdims=False
    )
    if grid.fast:
        block_output = grid.unpack(out_got, block_input, ties=[last_rows])

    summed = jnp.sum(exchange(last_rows, BOTH).astype(F32), axis=0)
    old_first = jnp.pad(square_momenta[0], ((0, each * grid.dp - local_chans), (0, 0)))
    old_first = lax.dynamic_slice_in_dim(old_first, lax.axis_index("dp") * each, each, axis=0)
    old_first = jnp.pad(MATRIX_MOMENTUM * old_first, ((0, row_count - each), (0, 0)))
    shared = share(lower(summed + old_first), BOTH)

    own_factor = orthogonal_factor(share_rows(mine_of_four), [shared])
    last_factor = orthogonal_factor(shared, (), each)
    if grid.fast:
        in_part = in_part.reshape(grid.count, local_chans, BLOCK)
        in_part = grid.move(behind(in_part, shared))
    else:
        in_part = grid.from_strips(in_part).astype(F32)
    early_factor = share_dp(behind(lower(own_factor), in_part))
    own_first = shared[:, :each].reshape(grid.dp, grid.chan, each, channels)
    own_first = lax.dynamic_index_in_dim(own_first, here, axis=1, keepdims=False)
    own_first = own_first.reshape(-1, channels)[:local_chans].astype(F32)
    last_sums = shared[:, each : each + few].reshape(-1, channels).astype(F32)

    def mine(rows, size):
        return lax.dynamic_slice_in_dim(rows, here * size, size, axis=-1)

    narrow_grad = mine(
        jnp.concatenate([last_sums[:8], branch_sums[5:6], branch_sums[4:5], last_sums[10:12]]),
        local_chans,
    )
    own_gain = narrow_vectors[0]
    slope_here = own_rstd * own_rstd * own_gain * narrow_grad[0] / pixel_count
    level_here = own_rstd * own_gain * narrow_grad[1] / pixel_count
    if grid.fast:
        coefs = jnp.stack([level_here, slope_here, own_mean])
        coefs = jnp.broadcast_to(coefs[:, :, None, None], coefs.shape + (1, LANES))
        input_grad = grid.unpack(in_part, cotangent, block_input, coefs)
    else:
        input_grad = (
            cotangent
            + in_part
            - level_here[:, None, None]
            - slope_here[:, None, None] * (block_input - own_mean[:, None, None])
        )

    new_square_momenta = jnp.stack([own_first, second_momentum, third_momentum])
    new_up_weight, new_down_weight, new_square_weights = vmem_call(
        functools.partial(
            finish_kernel,
            1.0 - MATRIX_RATE * WEIGHT_DECAY,
            MATRIX_RATE * math.sqrt(max(1.0, HID / C)),
        ),
        [
            jax.ShapeDtypeStruct(v.shape, F32) for v in (up_weight, down_weight, square_weights)
        ],
        [],
        4,
        "finish",
        early_factor,
        last_factor,
        new_up_momentum,
        down_rows,
        own_first,
        second_momentum,
        third_momentum,
        up_weight,
        down_weight,
        square_weights,
    )

    lka_grad = mine(last_sums[12:86], local_chans).T
    wide_grad, mlp_grad = side_grad[:, :2].T, side_grad[:, 2:]
    vector_step = VECTOR_RATE / math.sqrt(pixel_count)
    new_narrow_momenta = VECTOR_MOMENTUM * narrow_momenta + narrow_grad
    new_narrow_vectors = narrow_vectors - vector_step * new_narrow_momenta
    new_wide_momenta = VECTOR_MOMENTUM * wide_momenta + wide_grad
    new_wide_vectors = wide_vectors - vector_step * new_wide_momenta
    new_lka_momenta = VECTOR_MOMENTUM * lka_momenta + lka_grad
    new_lka_kernels = lka_kernels - vector_step * new_lka_momenta
    new_mlp_momentum = VECTOR_MOMENTUM * mlp_momentum + mlp_grad
    new_mlp_kernel = mlp_kernel - vector_step * new_mlp_momentum
    return (
        block_output,
        input_grad,
        new_square_weights,
        new_square_momenta,
        new_up_weight,
        new_up_momentum,
        new_down_weight,
        down_rows.T,
        new_narrow_vectors,
        new_narrow_momenta,
        new_wide_vectors,
        new_wide_momenta,
        new_lka_kernels,
        new_lka_momenta,
        new_mlp_kernel,
        new_mlp_momentum,
    )


def solution(mesh):
    placed = (
        P("chan", "dp", None),
        P("chan", "dp", None),
        P(),
        P(None, "chan", None),
        P(None, "chan", None),
        P("chan", None),
        P("chan", None),
        P(None, "chan"),
        P(None, "chan"),
        P(None, "chan"),
        P(None, "chan"),
        P(None, "chan"),
        P(None, "chan"),
        P("chan", None),
        P("chan", None),
        P("chan", None),
        P("chan", None),
    )
    return jax.shard_map(
        body,
        mesh=mesh,
        in_specs=placed,
        out_specs=(
            P("chan", "dp", None),
            P("chan", "dp", None),
            P(None, "chan", None),
            P(None, "chan", None),
            P("chan", None),
            P("chan", None),
            P(None, "chan"),
            P(None, "chan"),
            P(None, "chan"),
            P(None, "chan"),
            P(None, "chan"),
            P(None, "chan"),
            P("chan", None),
            P("chan", None),
            P("chan", None),
            P("chan", None),
        ),
        check_vma=False,
    )
```
